256 devices in a mesh: ns: 16 (over x_lo, y, core), ew: 16 (over x_hi, z).
Axes of the slice: x: 4 (x_hi: 2, x_lo: 2; x = x_hi * 2 + x_lo), y: 4, z: 8, core: 2. Of those that a mesh axis runs over, the one named last changes fastest.
Arguments:
- tokens: bfloat16 [512, 256, 1024], P('ns', 'ew'), may hold values from -6 to 6
- norm_gain: float32 [1024], replicated, may hold values from 0.5 to 1.5
- norm_bias: float32 [1024], replicated, may hold values from -2 to 2
- projection_weight: bfloat16 [1024, 3072], replicated, may hold values from -0.1875 to 0.1875
- projection_bias: float32 [3072], replicated, may hold values from -6 to 6
- context_gain: float32 [1024], replicated, may hold values from 0.5 to 1.5
- context_bias: float32 [1024], replicated, may hold values from -2 to 2
- output_weight: bfloat16 [1024, 1024], replicated, may hold values from -0.1875 to 0.1875
- output_bias: float32 [1024], replicated, may hold values from -2 to 2
- context_positions: int32 [256, 64], replicated, may hold values from 0 to 131071, as said below
Outputs:
- mixed: bfloat16 [512, 256, 1024], P('ns', 'ew')
- context: bfloat16 [256, 1024], replicated
The draws below stay inside these ranges and needn't reach their ends.
Inputs may be any that keep to these rules, and one draw needn't show every extreme that they name: `context_positions`: the positions of one context token all lie in one square of 16 x 16 grid tokens.
All inputs are finite; a program needn't handle non-finite values.
Results may differ from the reference program's by a relative error of at most 0.0049.
The reference program's roundings to bfloat16 on the way count: a program that leaves them out, or rounds other values in their place, can miss the bound.
Values may be sent and summed in bfloat16 or wider, within the bound.
A program may use at most 128 MiB of HBM per device.

```python
import jax
import jax.numpy as jnp
from jax import lax

D = 1024
HEADS = 16
RADIUS = 7
TH = 32
TW = 16
CTX = 256
POOL = 64
REGION = 16
GRID_NS = 512
GRID_EW = 256
N_NS = 16
N_EW = 16


def draw_projection_bias(key, part):
    key_base = jax.random.fold_in(key, 0)
    base_bias = jnp.clip(0.3 * jax.random.normal(key_base, (3 * D,), jnp.float32), -1.5, 1.5)
    return base_bias


def draw_context_positions(key, part):
    key_top, key_left, key_down, key_across = jax.random.split(key, 4)
    corner_row = jax.random.randint(key_top, (CTX, 1), 0, GRID_NS - REGION + 1)
    corner_col = jax.random.randint(key_left, (CTX, 1), 0, GRID_EW - REGION + 1)
    step_down = jax.random.randint(key_down, (CTX, POOL), 0, REGION)
    step_across = jax.random.randint(key_across, (CTX, POOL), 0, REGION)
    return ((corner_row + step_down) * GRID_EW + corner_col + step_across).astype(jnp.int32)


def level_of(own_key, dims, shards, smallest, top_value):
    factor_of = 1.0
    for position, shards_of in shards:
        steps = jax.random.uniform(jax.random.fold_in(jax.random.fold_in(own_key, 6), position), (shards_of,), jnp.float32, smallest / len(shards), top_value / len(shards))
        factor_of = factor_of * jnp.repeat(jnp.exp(steps), dims[position] // shards_of).reshape((-1,) + (1,) * (len(dims) - 1 - position))
    return factor_of


def centred(own_key, dims, scale, most, pieces=(), held_as=jnp.bfloat16):
    array = jax.random.normal(own_key, dims, jnp.float32) * scale
    if len(pieces) > 0:
        array = level_of(own_key, dims, pieces, -0.22, 0.18) * array
    return jnp.clip(array, min=-most, max=most).astype(held_as)


def setup_inputs(seed: int = 0) -> dict:
    seeds = jax.random.split(jax.random.key(seed), 11)
    tokens = centred(seeds[0], (GRID_NS, GRID_EW, D), 1.0, 6.0, ((0, 16), (1, 16)))
    norm_gain = jnp.clip(1.0 + 0.1 * jax.random.normal(seeds[1], (D,), jnp.float32), 0.5, 1.5)
    norm_bias = centred(seeds[2], (D,), 0.3, 2.0, (), jnp.float32)
    projection_weight = centred(seeds[3], (D, 3 * D), D ** -0.5, 0.1875)
    projection_bias = draw_projection_bias(jax.random.fold_in(seeds[10], 71), 0)
    context_gain = jnp.clip(1.0 + 0.1 * jax.random.normal(seeds[5], (D,), jnp.float32), 0.5, 1.5)
    context_bias = centred(seeds[6], (D,), 0.3, 2.0, (), jnp.float32)
    output_weight = centred(seeds[7], (D, D), D ** -0.5, 0.1875)
    output_bias = centred(seeds[8], (D,), 0.3, 2.0, (), jnp.float32)
    context_positions = draw_context_positions(jax.random.fold_in(seeds[10], 71), 0)
    return {"tokens": tokens, "norm_gain": norm_gain, "norm_bias": norm_bias, "projection_weight": projection_weight, "projection_bias": projection_bias, "context_gain": context_gain, "context_bias": context_bias, "output_weight": output_weight, "output_bias": output_bias, "context_positions": context_positions}


def layer_norm(inputs, gamma_gain, beta_bias):
    centre = inputs - lax.optimization_barrier(jnp.mean(inputs, axis=-1, keepdims=True))
    spread = lax.optimization_barrier(jnp.mean(centre * centre, axis=-1, keepdims=True))
    return centre * lax.rsqrt(spread + 1e-05) * gamma_gain + beta_bias

def neighbour_attention(queries, key_rim, value_rim, inside_mask, context_keys, context_values, head_count):
    tile_rows, tile_cols, features = queries.shape
    head_width = features // head_count
    window_span = key_rim.shape[0] - tile_rows + 1
    rim_cols = key_rim.shape[1]
    score_scale = head_width ** (-0.5)
    query_heads = queries.astype(jnp.float32).reshape(tile_rows, tile_cols, head_count, head_width)
    key_heads = key_rim.astype(jnp.float32).reshape(tile_rows + window_span - 1, rim_cols, head_count, head_width)
    value_heads = value_rim.astype(jnp.float32).reshape(tile_rows + window_span - 1, rim_cols, head_count, head_width)
    column_offset = lax.broadcasted_iota(jnp.int32, (rim_cols, tile_cols), 0) - lax.broadcasted_iota(jnp.int32, (rim_cols, tile_cols), 1)
    band_mask = (column_offset >= 0) & (column_offset < window_span)

    def near_score_row(row_shift):
        key_slab = lax.dynamic_slice_in_dim(key_heads, row_shift, tile_rows, 0)
        raw_scores = jnp.einsum('rxhd,rkhd->khrx', query_heads, key_slab) * score_scale
        inside_rows = lax.dynamic_slice_in_dim(inside_mask, row_shift, tile_rows, 0)
        keep_mask = band_mask[:, None, None, :] & jnp.transpose(inside_rows)[:, None, :, None]
        return jnp.where(keep_mask, raw_scores, -1e+30).reshape(rim_cols, head_count, tile_rows * tile_cols)
    near_scores = lax.map(near_score_row, jnp.arange(window_span, dtype=jnp.int32))
    context_heads_k = context_keys.astype(jnp.float32).reshape(-1, head_count, head_width)
    context_heads_v = context_values.astype(jnp.float32).reshape(-1, head_count, head_width)
    context_scores = jnp.einsum('rxhd,chd->chrx', query_heads, context_heads_k).reshape(-1, head_count, tile_rows * tile_cols) * score_scale
    row_maximum = jnp.maximum(lax.optimization_barrier(jnp.max(near_scores, axis=(0, 1))), lax.optimization_barrier(jnp.max(context_scores, axis=0)))
    near_exp = jnp.exp(near_scores - row_maximum)
    context_exp = jnp.exp(context_scores - row_maximum)
    denominator = lax.optimization_barrier(jnp.sum(near_exp, axis=(0, 1))) + lax.optimization_barrier(jnp.sum(context_exp, axis=0))
    near_weights = near_exp.astype(jnp.bfloat16).reshape(window_span, rim_cols, head_count, tile_rows, tile_cols)
    context_weights = context_exp.astype(jnp.bfloat16).reshape(-1, head_count, tile_rows, tile_cols)

    def add_values(running, shift_pair):
        row_shift, row_weights = shift_pair
        value_slab = lax.dynamic_slice_in_dim(value_heads, row_shift, tile_rows, 0)
        return (running + jnp.einsum('khrx,rkhd->rxhd', row_weights.astype(jnp.float32), value_slab), None)
    context_sum = jnp.einsum('chrx,chd->rxhd', context_weights.astype(jnp.float32), context_heads_v)
    summed, ignored = lax.scan(add_values, context_sum, (jnp.arange(window_span, dtype=jnp.int32), near_weights))
    divisor = jnp.transpose(denominator.reshape(head_count, tile_rows, tile_cols), (1, 2, 0))[..., None]
    return (summed / divisor).astype(jnp.bfloat16).reshape(tile_rows, tile_cols, features)

def reference(tokens, norm_gain, norm_bias, projection_weight, projection_bias, context_gain, context_bias, output_weight, output_bias, context_positions):
    features = D
    flat_tokens = tokens.reshape(-1, features)
    pair_weight = projection_weight[:, features:]
    pair_bias = projection_bias[features:]

    def band_normed(token_band):
        return layer_norm(token_band.astype(jnp.float32), norm_gain, norm_bias).astype(jnp.bfloat16)
    normed = lax.map(band_normed, tokens.reshape(N_NS, TH, GRID_EW, features)).reshape(GRID_NS, GRID_EW, features)

    def band_pairs(normed_band):
        projected = jnp.dot(normed_band.reshape(-1, features), pair_weight, preferred_element_type=jnp.float32) + pair_bias
        return projected.astype(jnp.bfloat16).reshape(TH, GRID_EW, 2 * features)
    pair_values = lax.map(band_pairs, normed.reshape(N_NS, TH, GRID_EW, features)).reshape(GRID_NS, GRID_EW, 2 * features)
    padded = jnp.pad(pair_values, ((RADIUS, RADIUS), (RADIUS, RADIUS), (0, 0)))
    inside = jnp.pad(jnp.ones((GRID_NS, GRID_EW), dtype=bool), RADIUS)
    picked_tokens = flat_tokens[context_positions.reshape(-1).astype(jnp.int32)].astype(jnp.float32)
    pooled = lax.optimization_barrier(jnp.sum(picked_tokens.reshape(CTX, POOL, features), axis=1))
    context = layer_norm(pooled, context_gain, context_bias).astype(jnp.bfloat16)
    context_pairs = (jnp.dot(context, pair_weight, preferred_element_type=jnp.float32) + pair_bias).astype(jnp.bfloat16)
    context_keys = context_pairs[:, :features]
    context_values = context_pairs[:, features:]
    zero_index = jnp.int32(0)

    def one_tile(tile_index):
        first_row = tile_index // N_EW * TH
        first_col = tile_index % N_EW * TW
        token_block = lax.dynamic_slice(normed, (first_row, first_col, zero_index), (TH, TW, features))
        queries = jnp.dot(token_block.reshape(-1, features), projection_weight[:, :features], preferred_element_type=jnp.float32) + projection_bias[:features]
        queries = queries.astype(jnp.bfloat16).reshape(TH, TW, features)
        pair_rim = lax.dynamic_slice(padded, (first_row, first_col, zero_index), (TH + 2 * RADIUS, TW + 2 * RADIUS, 2 * features))
        inside_mask = lax.dynamic_slice(inside, (first_row, first_col), (TH + 2 * RADIUS, TW + 2 * RADIUS))
        attended = neighbour_attention(queries, pair_rim[..., :features], pair_rim[..., features:], inside_mask, context_keys, context_values, HEADS)
        own_tokens = lax.dynamic_slice(tokens, (first_row, first_col, zero_index), (TH, TW, features))
        mixed_out = own_tokens.reshape(-1, features).astype(jnp.float32) + jnp.dot(attended.reshape(-1, features), output_weight, preferred_element_type=jnp.float32) + output_bias
        return mixed_out.astype(jnp.bfloat16).reshape(TH, TW, features)
    tile_outputs = lax.map(one_tile, jnp.arange(N_NS * N_EW, dtype=jnp.int32))
    mixed = jnp.transpose(tile_outputs.reshape(N_NS, N_EW, TH, TW, features), (0, 2, 1, 3, 4)).reshape(GRID_NS, GRID_EW, features)
    return (mixed, context)
```

```python
import functools
import jax
import jax.numpy as jnp
from jax import lax
from jax.experimental import pallas as pl
from jax.experimental.pallas import tpu as pltpu
from jax.sharding import PartitionSpec as P

F32 = jnp.float32
BF16 = jnp.bfloat16
NT = (((1,), (1,)), ((), ()))


def norm_rows(x, gain, bias):
    centre = x - jnp.mean(x, axis=-1, keepdims=True)
    spread = jnp.mean(centre * centre, axis=-1, keepdims=True)
    return centre * lax.rsqrt(spread + 1e-05) * gain + bias


def compute(unroll, place_ref, rim, ctx, gain, beta, w, wb, wo, ob, out,
            wq_v, wk_v, wv_v, wo_v, normed, k, v, kc, vc, q2, att, near_bias, s_buf, p_buf, sem):
    copies = [
        pltpu.make_async_copy(w.at[:, pl.ds(1024, 1024)], wk_v, sem.at[0]),
        pltpu.make_async_copy(w.at[:, pl.ds(2048, 1024)], wv_v, sem.at[1]),
        pltpu.make_async_copy(w.at[:, pl.ds(0, 1024)], wq_v, sem.at[2]),
        pltpu.make_async_copy(wo, wo_v, sem.at[3]),
    ]
    for c in copies:
        c.start()
    row0 = place_ref[0] * 32
    col0 = place_ref[1] * 16

    @pl.loop(0, 12)
    def _(t):
        rows = pl.ds(pl.multiple_of(t * 128, 128), 128)
        normed[rows, :] = norm_rows(rim[rows, :].astype(F32), gain[...], beta[...]).astype(BF16)

    def project(src, dst, weight, bias_at, m, tile):
        @pl.loop(0, m // tile)
        def _(t):
            rows = pl.ds(pl.multiple_of(t * tile, tile), tile)
            for n in range(2):
                cols = slice(n * 512, n * 512 + 512)
                y = jnp.dot(src[rows, :], weight[:, cols], preferred_element_type=F32)
                y = y + wb[:, bias_at + n * 512:bias_at + n * 512 + 512]
                dst[rows, cols] = y.astype(BF16)

    copies[0].wait()
    project(normed, k, wk_v, 1024, 1536, 512)
    project(ctx, kc, wk_v, 1024, 256, 256)
    copies[1].wait()
    project(normed, v, wv_v, 2048, 1536, 512)
    project(ctx, vc, wv_v, 2048, 256, 256)
    copies[2].wait()
    low = lax.broadcasted_iota(jnp.int32, (128, 128), 1) < 64

    @pl.loop(0, 4)
    def _(b):
        rows = pl.ds(pl.multiple_of(b * 256 + 256, 256), 128)
        for n in range(2):
            y = jnp.dot(normed[rows, :], wq_v[:, n * 512:n * 512 + 512], preferred_element_type=F32)
            y = (y + wb[:, n * 512:n * 512 + 512]).astype(BF16).astype(F32) * 0.125
            for i in range(4):
                q = y[:, i * 128:i * 128 + 128]
                q2[b, n * 4 + i, 0:128, :] = jnp.where(low, q, 0.0).astype(BF16)
                q2[b, n * 4 + i, 128:256, :] = jnp.where(low, 0.0, q).astype(BF16)

    copies[3].wait()

    @pl.loop(0, 4)
    def _(b):
        for j in range(6):
            qi = lax.broadcasted_iota(jnp.int32, (128, 128), 0)
            ki = lax.broadcasted_iota(jnp.int32, (128, 128), 1)
            qr = 8 + qi // 16
            qc = 8 + qi % 16
            if j % 2 == 0:
                kr = 8 * (j // 2) + ki // 16
                kc_ = 8 + ki % 16
            else:
                kr = 8 * (j // 2) + (ki % 64) // 8
                kc_ = ki % 8 + jnp.where(ki < 64, 0, 24)
            gr = row0 + 8 * b - 8 + kr
            gc = col0 - 8 + kc_
            ok = ((kr - qr <= 7) & (qr - kr <= 7) & (kc_ - qc <= 7) & (qc - kc_ <= 7)
                  & (gr >= 0) & (gr < 512) & (gc >= 0) & (gc < 256))
            near_bias[:, j * 128:j * 128 + 128] = jnp.where(ok, 0.0, -1e30)

        slab = pl.ds(pl.multiple_of(b * 256, 256), 768)
        qrows = pl.ds(pl.multiple_of(b * 128, 128), 128)

        @pl.loop(0, 8 // unroll)
        def _(po):
            for u in range(unroll):
                p = po * unroll + u
                lanes = pl.ds(pl.multiple_of(p * 128, 128), 128)
                s_ref = s_buf.at[u]
                p_ref = p_buf.at[u]
                q = q2[b, p]
                s_ref[:, 0:256] = lax.dot_general(q, kc[:, lanes], NT, preferred_element_type=F32)
                s_ref[:, 256:1024] = lax.dot_general(q, k[slab, lanes], NT, preferred_element_type=F32)
                ls = []
                for r in range(16):
                    rows = slice(r * 16, r * 16 + 16)
                    mrows = slice((r % 8) * 16, (r % 8) * 16 + 16)
                    sc = s_ref[rows, 0:256]
                    sn = s_ref[rows, 256:1024] + near_bias[mrows, :]
                    s = jnp.concatenate([sc, sn], axis=1)
                    m = jnp.max(s, axis=1, keepdims=True)
                    e = jnp.exp(s - m)
                    ls.append(jnp.sum(e, axis=1, keepdims=True))
                    p_ref[rows, :] = e.astype(BF16)
                o = jnp.dot(p_ref[:, 0:256], vc[:, lanes], preferred_element_type=F32)
                o = o + jnp.dot(p_ref[:, 256:1024], v[slab, lanes], preferred_element_type=F32)
                l = jnp.concatenate(ls, axis=0)
                o = o / l
                att[qrows, lanes] = jnp.where(low, o[0:128], o[128:256]).astype(BF16)

    @pl.loop(0, 4)
    def _(b):
        rows = pl.ds(pl.multiple_of(b * 128, 128), 128)
        src = pl.ds(pl.multiple_of(b * 256 + 256, 256), 128)
        for n in range(2):
            cols = slice(n * 512, n * 512 + 512)
            y = jnp.dot(att[rows, :], wo_v[:, cols], preferred_element_type=F32)
            out[rows, cols] = (rim[src, cols].astype(F32) + y + ob[:, cols]).astype(BF16)


def compute_call(place, rim, ctx, gain, beta, w, wb, wo, ob, unroll=2):
    vm = pl.BlockSpec(memory_space=pltpu.VMEM)
    anyspec = pl.BlockSpec(memory_space=pl.ANY)
    return pl.pallas_call(
        functools.partial(compute, unroll),
        out_shape=jax.ShapeDtypeStruct((512, 1024), BF16),
        in_specs=[pl.BlockSpec(memory_space=pltpu.SMEM), vm, vm, vm, vm, anyspec, vm, anyspec, vm],
        out_specs=vm,
        scratch_shapes=[pltpu.VMEM((1024, 1024), BF16)] * 4 + [
            pltpu.VMEM((1536, 1024), BF16), pltpu.VMEM((1536, 1024), BF16), pltpu.VMEM((1536, 1024), BF16),
            pltpu.VMEM((256, 1024), BF16), pltpu.VMEM((256, 1024), BF16),
            pltpu.VMEM((4, 8, 256, 128), BF16), pltpu.VMEM((512, 1024), BF16),
            pltpu.VMEM((128, 768), F32), pltpu.VMEM((unroll, 256, 1024), F32), pltpu.VMEM((unroll, 256, 1024), BF16),
            pltpu.SemaphoreType.DMA((4,)),
        ],
        compiler_params=pltpu.CompilerParams(vmem_limit_bytes=56 * 2**20),
        name="attend",
    )(place, rim, ctx, gain.reshape(1, -1), beta.reshape(1, -1), w, wb.reshape(1, -1), wo, ob.reshape(1, -1))


MESH = pl.DeviceIdType.MESH


def exchange(tokens, pos, cgain, cbias, rim, ctx,
             send_l, send_r, counts, partial, buf0, p1, buf1, p2, buf2, g,
             halo_s, halo_r, s0, r0, s1, r1, s2, r2, s3, r3, s4, r4):
    ns = lax.axis_index("ns")
    ew = lax.axis_index("ew")
    core = lax.rem(ns, 2)
    unit = ns // 2

    barrier = pltpu.get_barrier_semaphore()

    @pl.loop(1, 16)
    def _(d):
        pl.semaphore_signal(barrier, inc=1, device_id=(lax.rem(ns + d, 16), ew), device_id_type=MESH)
        pl.semaphore_signal(barrier, inc=1, device_id=(ns, lax.rem(ew + d, 16)), device_id_type=MESH)

    @pl.loop(0, 4)
    def _(b):
        x = tokens[pl.ds(pl.multiple_of(b * 128, 128), 128), :]
        rim[b + 1, 0:128, :] = x
        x = x.astype(F32).reshape(8, 2, 8, 1024)
        send_l[b] = x[:, 0].reshape(64, 1024).astype(BF16)
        send_r[b] = x[:, 1].reshape(64, 1024).astype(BF16)

    pl.semaphore_wait(barrier, 30)

    up, down, left, right = (ns - 1, ew), (ns + 1, ew), (ns, ew - 1), (ns, ew + 1)

    def halo(i, src, dst, device):
        return pltpu.make_async_remote_copy(src_ref=src, dst_ref=dst, send_sem=halo_s.at[i], recv_sem=halo_r.at[i],
                                            device_id=device, device_id_type=MESH)
    mid = pl.ds(1, 4)
    go_left = halo(0, send_l, rim.at[mid, pl.ds(192, 64)], left)
    go_right = halo(1, send_r, rim.at[mid, pl.ds(128, 64)], right)
    go_up = halo(2, tokens.at[pl.ds(0, 128)], rim.at[5, pl.ds(0, 128)], up)
    go_down = halo(3, tokens.at[pl.ds(384, 128)], rim.at[0, pl.ds(0, 128)], down)
    corner = {}
    for k, at in ((0, 128), (1, 192)):
        corner[k] = (halo(4 + 2 * k, rim.at[1, pl.ds(at, 64)], rim.at[5, pl.ds(at, 64)], up),
                     halo(5 + 2 * k, rim.at[4, pl.ds(at, 64)], rim.at[0, pl.ds(at, 64)], down))
    has_up, has_down, has_left, has_right = ns > 0, ns < 15, ew > 0, ew < 15
    pl.when(has_left)(go_left.start)
    pl.when(has_right)(go_right.start)
    pl.when(has_up)(go_up.start)
    pl.when(has_down)(go_down.start)

    @pl.when(jnp.logical_not(has_up))
    def _():
        rim[0] = jnp.zeros((256, 1024), BF16)

    @pl.when(jnp.logical_not(has_down))
    def _():
        rim[5] = jnp.zeros((256, 1024), BF16)

    for gone, at in ((ew == 0, 128), (ew == 15, 192)):
        @pl.when(gone)
        def _():
            @pl.loop(0, 6)
            def _(t):
                rim[t, at:at + 64, :] = jnp.zeros((64, 1024), BF16)

    def count(t):
        rows = pl.ds(pl.multiple_of(t * 32, 32), 32)
        at = pos[rows, :]
        lr = (at >> 8) - ns * 32
        lc = (at & 255) - ew * 16
        own = (lr >= 0) & (lr < 32) & (lc >= 0) & (lc < 16)
        own_id = jnp.where(own, lr * 16 + lc, -1)
        ids = lax.broadcasted_iota(jnp.int32, (32, 512), 1)
        total = jnp.zeros((32, 512), F32)
        for p in range(64):
            total = total + jnp.where(own_id[:, p:p + 1] == ids, 1.0, 0.0)
        counts[rows, :] = total.astype(BF16)

    pl.loop(0, 8)(count)

    @pl.loop(0, 2)
    def _(t):
        rows = pl.ds(pl.multiple_of(t * 128, 128), 128)
        for n in range(2):
            cols = slice(n * 512, n * 512 + 512)
            partial[rows, cols] = jnp.dot(counts[rows, :], tokens[:, cols], preferred_element_type=F32)

    pair = pltpu.make_async_remote_copy(
        src_ref=partial.at[pl.ds(pl.multiple_of((1 - core) * 128, 128), 128)], dst_ref=buf0, send_sem=s0, recv_sem=r0,
        device_id=(ns + 1 - 2 * core, ew), device_id_type=MESH)
    pair.start()
    pair.wait()

    @pl.loop(0, 8)
    def _(t):
        p1[t] = (partial[pl.ds(pl.multiple_of(core * 128 + t * 16, 16), 16), :]
                 + buf0[pl.ds(pl.multiple_of(t * 16, 16), 16), :])

    def stage1(d):
        to = lax.rem(unit + d, 8)
        return pltpu.make_async_remote_copy(src_ref=p1.at[to], dst_ref=buf1.at[d], send_sem=s1.at[d], recv_sem=r1.at[d],
                                            device_id=(to * 2 + core, ew), device_id_type=MESH)
    pl.loop(1, 8)(lambda d: stage1(d).start())
    pl.loop(1, 8)(lambda d: stage1(d).wait())
    total = p1[unit]
    for d in range(1, 8):
        total = total + buf1[d]
    for i in range(8):
        p2[:, i, :] = total[:, i * 128:i * 128 + 128]

    def stage2(d):
        to = lax.rem(ew + d, 16)
        return pltpu.make_async_remote_copy(src_ref=p2.at[to], dst_ref=buf2.at[d], send_sem=s2.at[d], recv_sem=r2.at[d],
                                            device_id=(ns, to), device_id_type=MESH)
    pl.loop(1, 16)(lambda d: stage2(d).start())
    pl.loop(1, 16)(lambda d: stage2(d).wait())
    total = p2[ew]
    for d in range(1, 16):
        total = total + buf2[d]
    g[ew] = total

    def stage3(d):
        return pltpu.make_async_remote_copy(src_ref=g.at[ew], dst_ref=g.at[ew], send_sem=s3.at[d], recv_sem=r3.at[d],
                                            device_id=(ns, lax.rem(ew + d, 16)), device_id_type=MESH)

    def stage3_in(d):
        at = lax.rem(ew + 16 - d, 16)
        return pltpu.make_async_remote_copy(src_ref=g.at[at], dst_ref=g.at[at], send_sem=s3.at[d], recv_sem=r3.at[d],
                                            device_id=(ns, at), device_id_type=MESH)
    pl.loop(1, 16)(lambda d: stage3(d).start())

    for k, came in ((0, has_left), (1, has_right)):
        @pl.when(came)
        def _():
            (go_right, go_left)[k].wait_recv()
            pl.when(has_up)(corner[k][0].start)
            pl.when(has_down)(corner[k][1].start)

    @pl.loop(1, 16)
    def _(d):
        stage3(d).wait_send()
        stage3_in(d).wait_recv()

    pooled = jnp.concatenate([g[:, i, :] for i in range(8)], axis=1)
    ctx[core, unit] = norm_rows(pooled, cgain[...], cbias[...]).astype(BF16)

    def stage4(d):
        to = lax.rem(ns + d, 16)
        mine = ctx.at[core, unit]
        return pltpu.make_async_remote_copy(src_ref=mine, dst_ref=mine, send_sem=s4.at[d], recv_sem=r4.at[d],
                                            device_id=(to, ew), device_id_type=MESH)

    def stage4_in(d):
        at = lax.rem(ns + 16 - d, 16)
        theirs = ctx.at[lax.rem(at, 2), at // 2]
        return pltpu.make_async_remote_copy(src_ref=theirs, dst_ref=theirs, send_sem=s4.at[d], recv_sem=r4.at[d],
                                            device_id=(at, ew), device_id_type=MESH)
    pl.loop(1, 16)(lambda d: stage4(d).start())

    @pl.loop(1, 16)
    def _(d):
        stage4(d).wait_send()
        stage4_in(d).wait_recv()

    pl.when(has_left)(go_left.wait_send)
    pl.when(has_right)(go_right.wait_send)
    pl.when(has_up)(go_up.wait_send)
    pl.when(has_down)(go_down.wait_send)
    pl.when(has_down)(go_up.wait_recv)
    pl.when(has_up)(go_down.wait_recv)
    for k, came in ((0, has_left), (1, has_right)):
        pl.when(came & has_up)(corner[k][0].wait_send)
        pl.when(came & has_down)(corner[k][1].wait_send)
        pl.when(came & has_down)(corner[k][0].wait_recv)
        pl.when(came & has_up)(corner[k][1].wait_recv)


def exchange_call(tokens, pos, cgain, cbias):
    vm = pl.BlockSpec(memory_space=pltpu.VMEM)
    dma = pltpu.SemaphoreType.DMA
    return pl.pallas_call(
        exchange,
        out_shape=(jax.ShapeDtypeStruct((6, 256, 1024), BF16), jax.ShapeDtypeStruct((2, 8, 16, 1024), BF16)),
        in_specs=[vm] * 4,
        out_specs=(vm, vm),
        scratch_shapes=[
            pltpu.VMEM((4, 64, 1024), BF16), pltpu.VMEM((4, 64, 1024), BF16),
            pltpu.VMEM((256, 512), BF16), pltpu.VMEM((256, 1024), F32),
            pltpu.VMEM((128, 1024), F32), pltpu.VMEM((8, 16, 1024), F32), pltpu.VMEM((8, 16, 1024), F32),
            pltpu.VMEM((16, 8, 128), F32), pltpu.VMEM((16, 8, 128), F32), pltpu.VMEM((16, 8, 128), F32),
            dma((8,)), dma((8,)), dma, dma, dma((8,)), dma((8,)),
            dma((16,)), dma((16,)), dma((16,)), dma((16,)), dma((16,)), dma((16,)),
        ],
        compiler_params=pltpu.CompilerParams(collective_id=0, has_side_effects=True, vmem_limit_bytes=40 * 2**20),
        name="exchange",
    )(tokens, pos, cgain.reshape(1, -1), cbias.reshape(1, -1))


def on_device(tokens, norm_gain, norm_bias, projection_weight, projection_bias, context_gain, context_bias,
              output_weight, output_bias, context_positions):
    flat = tokens.reshape(512, 1024)
    rim, ctx = exchange_call(flat, context_positions, context_gain, context_bias)
    context = ctx.reshape(256, 1024)
    place = jnp.stack([lax.axis_index("ns"), lax.axis_index("ew")]).astype(jnp.int32)
    mixed = compute_call(place, rim.reshape(1536, 1024), context, norm_gain, norm_bias, projection_weight,
                         projection_bias, output_weight, output_bias)
    return mixed.reshape(32, 16, 1024), context


def solution(mesh):
    return jax.shard_map(
        on_device,
        mesh=mesh,
        in_specs=(P("ns", "ew", None), P(), P(), P(), P(), P(), P(), P(), P(), P()),
        out_specs=(P("ns", "ew", None), P()),
        check_vma=False,
    )
```

```python
import jax
import jax.numpy as jnp
from jax import lax
from jax.experimental import pallas as pl
from jax.experimental.pallas import tpu as pltpu
from jax.sharding import PartitionSpec as P

F32 = jnp.float32
BF16 = jnp.bfloat16
MESH = pl.DeviceIdType.MESH
NT = (((1,), (1,)), ((), ()))
TN = (((0,), (0,)), ((), ()))


def rows_at(start, size):
    return pl.ds(pl.multiple_of(start, size), size)


def norm_rows(x, gain, bias):
    centre = x - jnp.mean(x, axis=-1, keepdims=True)
    spread = jnp.mean(centre * centre, axis=-1, keepdims=True)
    return centre * lax.rsqrt(spread + 1e-05) * gain + bias


def layer(tokens_hbm, pos_hbm, w_hbm, wo_hbm, gain, beta, wb, cgain, cbias, ob, out, ctx_out,
          tokens, pos, wq, wk, wv, wo, normed, k, v, q2, att, near_o, near_m, near_l, near_bias,
          s_a, s_b, p_a, p_b, ml_a, ml_b, cs, cp, cml, kc, vc, ctx,
          rim, send_l, send_r, counts, partial, buf0, p1, buf1, p2, buf2, g,
          load, halo_s, halo_r, s0, r0, s1, r1, s2, r2, s3, r3, s4, r4):
    ns = lax.axis_index("ns")
    ew = lax.axis_index("ew")
    core = lax.rem(ns, 2)
    unit = ns // 2

    barrier = pltpu.get_barrier_semaphore()

    @pl.loop(1, 16)
    def _(d):
        pl.semaphore_signal(barrier, inc=1, device_id=(lax.rem(ns + d, 16), ew), device_id_type=MESH)
        pl.semaphore_signal(barrier, inc=1, device_id=(ns, lax.rem(ew + d, 16)), device_id_type=MESH)

    loads = [pltpu.make_async_copy(a, b, load.at[i]) for i, (a, b) in enumerate((
        (tokens_hbm, tokens), (pos_hbm, pos), (w_hbm.at[:, pl.ds(1024, 1024)], wk), (w_hbm.at[:, pl.ds(2048, 1024)], wv),
        (w_hbm.at[:, pl.ds(0, 1024)], wq), (wo_hbm, wo)))]
    for c in loads:
        c.start()
    loads[0].wait()

    @pl.loop(0, 4)
    def _(b):
        x = tokens[rows_at(b * 128, 128), :].astype(F32).reshape(8, 2, 8, 1024)
        send_l[b] = x[:, 0].reshape(64, 1024).astype(BF16)
        send_r[b] = x[:, 1].reshape(64, 1024).astype(BF16)

    up, down, left, right = (ns - 1, ew), (ns + 1, ew), (ns, ew - 1), (ns, ew + 1)

    def halo(i, src, dst, device):
        return pltpu.make_async_remote_copy(src_ref=src, dst_ref=dst, send_sem=halo_s.at[i], recv_sem=halo_r.at[i],
                                            device_id=device, device_id_type=MESH)
    west, east = pl.ds(128, 64), pl.ds(192, 64)
    go_left = [halo(0, send_l.at[0], rim.at[1, east], left), halo(1, send_l.at[3], rim.at[4, east], left),
               halo(2, send_l.at[pl.ds(1, 2)], rim.at[pl.ds(2, 2), east], left)]
    go_right = [halo(3, send_r.at[0], rim.at[1, west], right), halo(4, send_r.at[3], rim.at[4, west], right),
                halo(5, send_r.at[pl.ds(1, 2)], rim.at[pl.ds(2, 2), west], right)]
    go_up = [halo(6, tokens.at[pl.ds(0, 128)], rim.at[5, pl.ds(0, 128)], up)]
    go_down = [halo(7, tokens.at[pl.ds(384, 128)], rim.at[0, pl.ds(0, 128)], down)]
    west_up = halo(8, rim.at[1, west], rim.at[5, west], up)
    west_down = halo(9, rim.at[4, west], rim.at[0, west], down)
    east_up = halo(10, rim.at[1, east], rim.at[5, east], up)
    east_down = halo(11, rim.at[4, east], rim.at[0, east], down)
    has_up, has_down, has_left, has_right = ns > 0, ns < 15, ew > 0, ew < 15

    def when_all(cond, calls):
        @pl.when(cond)
        def _():
            for c in calls:
                c()

    pl.semaphore_wait(barrier, 30)
    for i in range(3):
        pl.when(has_left)(go_left[i].start)
        pl.when(has_right)(go_right[i].start)
    pl.when(has_up)(go_up[0].start)
    pl.when(has_down)(go_down[0].start)

    @pl.when(jnp.logical_not(has_up))
    def _():
        rim[0] = jnp.zeros((256, 1024), BF16)

    @pl.when(jnp.logical_not(has_down))
    def _():
        rim[5] = jnp.zeros((256, 1024), BF16)

    for gone, at in ((ew == 0, 128), (ew == 15, 192)):
        @pl.when(gone)
        def _():
            @pl.loop(0, 6)
            def _(t):
                rim[t, at:at + 64, :] = jnp.zeros((64, 1024), BF16)

    loads[1].wait()

    @pl.loop(0, 8)
    def _(t):
        at = pos[...]
        lr = (at >> 8) - ns * 32
        lc = (at & 255) - ew * 16
        own = (lr >= 0) & (lr < 32) & (lc >= 0) & (lc < 16)
        own_id = jnp.where(own, lr * 16 + lc, -1)
        ids = lax.broadcasted_iota(jnp.int32, (64, 256), 0) + t * 64
        total = jnp.zeros((64, 256), F32)
        for p in range(64):
            total = total + jnp.where(own_id[p:p + 1, :] == ids, 1.0, 0.0)
        counts[rows_at(t * 64, 64), :] = total.astype(BF16)

    @pl.loop(0, 4)
    def _(t):
        cols = rows_at(t * 256, 256)
        partial[:, cols] = lax.dot_general(counts[...], tokens[:, cols], TN, preferred_element_type=F32)

    pair = pltpu.make_async_remote_copy(
        src_ref=partial.at[rows_at((1 - core) * 128, 128)], dst_ref=buf0, send_sem=s0, recv_sem=r0,
        device_id=(ns + 1 - 2 * core, ew), device_id_type=MESH)
    pair.start()

    def project(weight, bias_at, dst, place):
        @pl.loop(0, 4)
        def _(n):
            cols = rows_at(n * 256, 256)
            y = jnp.dot(normed[...], weight[:, cols], preferred_element_type=F32)
            y = (y + wb[:, rows_at(bias_at + n * 256, 256)]).astype(BF16)
            for i in range(4):
                dst[place[i]:place[i] + 128, cols] = y[i * 128:i * 128 + 128]

    @pl.loop(0, 4)
    def _(i):
        rows = rows_at(i * 128, 128)
        normed[rows, :] = norm_rows(tokens[rows, :].astype(F32), gain[...], beta[...]).astype(BF16)

    mid_own = (256, 512, 768, 1024)
    mid_side = (384, 640, 896, 1152)
    loads[2].wait()
    project(wk, 1024, k, mid_own)
    loads[3].wait()
    project(wv, 2048, v, mid_own)

    pair.wait()

    @pl.loop(0, 8)
    def _(t):
        p1[t] = partial[rows_at(core * 128 + t * 16, 16), :] + buf0[rows_at(t * 16, 16), :]

    def stage1(d):
        to = lax.rem(unit + d, 8)
        return pltpu.make_async_remote_copy(src_ref=p1.at[to], dst_ref=buf1.at[d], send_sem=s1.at[d], recv_sem=r1.at[d],
                                            device_id=(to * 2 + core, ew), device_id_type=MESH)
    pl.loop(1, 8)(lambda d: stage1(d).start())

    low = lax.broadcasted_iota(jnp.int32, (128, 128), 1) < 64
    loads[4].wait()

    @pl.loop(0, 4)
    def _(n):
        cols = rows_at(n * 256, 256)
        y = jnp.dot(normed[...], wq[:, cols], preferred_element_type=F32)
        y = (y + wb[:, cols]).astype(BF16).astype(F32) * 0.125
        for b in range(4):
            for i in range(2):
                q = y[b * 128:b * 128 + 128, i * 128:i * 128 + 128]
                q2[n * 2 + i, b * 256:b * 256 + 128, :] = jnp.where(low, q, 0.0).astype(BF16)
                q2[n * 2 + i, b * 256 + 128:b * 256 + 256, :] = jnp.where(low, 0.0, q).astype(BF16)

    for i in range(2):
        pl.when(has_left)(go_right[i].wait_recv)
        pl.when(has_right)(go_left[i].wait_recv)
    when_all(has_left & has_up, [west_up.start])
    when_all(has_left & has_down, [west_down.start])
    when_all(has_right & has_up, [east_up.start])
    when_all(has_right & has_down, [east_down.start])
    pl.when(has_left)(go_right[2].wait_recv)
    pl.when(has_right)(go_left[2].wait_recv)

    @pl.loop(0, 4)
    def _(i):
        normed[rows_at(i * 128, 128), :] = norm_rows(
            rim[i + 1, 128:256, :].astype(F32), gain[...], beta[...]).astype(BF16)

    project(wk, 1024, k, mid_side)

    pl.loop(1, 8)(lambda d: stage1(d).wait())
    total = p1[unit]
    for d in range(1, 8):
        total = total + buf1[d]
    for i in range(8):
        p2[:, i, :] = total[:, i * 128:i * 128 + 128]

    def stage2(d):
        to = lax.rem(ew + d, 16)
        return pltpu.make_async_remote_copy(src_ref=p2.at[to], dst_ref=buf2.at[d], send_sem=s2.at[d], recv_sem=r2.at[d],
                                            device_id=(ns, to), device_id_type=MESH)
    pl.loop(1, 16)(lambda d: stage2(d).start())

    project(wv, 2048, v, mid_side)

    def stage3(d):
        return pltpu.make_async_remote_copy(src_ref=g.at[ew], dst_ref=g.at[ew], send_sem=s3.at[d], recv_sem=r3.at[d],
                                            device_id=(ns, lax.rem(ew + d, 16)), device_id_type=MESH)

    def stage3_in(d):
        at = lax.rem(ew + 16 - d, 16)
        return pltpu.make_async_remote_copy(src_ref=g.at[at], dst_ref=g.at[at], send_sem=s3.at[d], recv_sem=r3.at[d],
                                            device_id=(ns, at), device_id_type=MESH)

    def stage4(d):
        mine = ctx.at[core, unit]
        return pltpu.make_async_remote_copy(src_ref=mine, dst_ref=mine, send_sem=s4.at[d], recv_sem=r4.at[d],
                                            device_id=(lax.rem(ns + d, 16), ew), device_id_type=MESH)

    def stage4_in(d):
        at = lax.rem(ns + 16 - d, 16)
        theirs = ctx.at[lax.rem(at, 2), at // 2]
        return pltpu.make_async_remote_copy(src_ref=theirs, dst_ref=theirs, send_sem=s4.at[d], recv_sem=r4.at[d],
                                            device_id=(at, ew), device_id_type=MESH)

    s_buf, p_buf, ml_buf = (s_a, s_b), (p_a, p_b), (ml_a, ml_b)

    def soft_rows(s, bias, pb, mlb, at, size):
        rows = slice(at, at + size)
        x = s[rows, :]
        if bias is not None:
            x = x + bias[at % 128:at % 128 + size, :]
        m = jnp.max(x, axis=1, keepdims=True)
        e = jnp.exp(x - m)
        l = jnp.sum(e, axis=1, keepdims=True)
        pb[rows, :] = e.astype(BF16)
        mlb[0, rows, :] = jnp.broadcast_to(m, (size, 128))
        mlb[1, rows, :] = jnp.broadcast_to(l, (size, 128))

    def band_step(t):
        b = lax.rem(t + 1, 4)
        for j in range(6):
            qi = lax.broadcasted_iota(jnp.int32, (128, 128), 0)
            ki = lax.broadcasted_iota(jnp.int32, (128, 128), 1)
            qr = 8 + qi // 16
            qc = 8 + qi % 16
            if j % 2 == 0:
                kr = 8 * (j // 2) + ki // 16
                kc_ = 8 + ki % 16
            else:
                kr = 8 * (j // 2) + (ki % 64) // 8
                kc_ = ki % 8 + jnp.where(ki < 64, 0, 24)
            gr = ns * 32 + 8 * b - 8 + kr
            gc = ew * 16 - 8 + kc_
            ok = ((kr - qr <= 7) & (qr - kr <= 7) & (kc_ - qc <= 7) & (qc - kc_ <= 7)
                  & (gr >= 0) & (gr < 512) & (gc >= 0) & (gc < 256))
            near_bias[:, j * 128:j * 128 + 128] = jnp.where(ok, 0.0, -1e30)

        qrows = rows_at(b * 128, 128)

        def keys(part):
            return rows_at(b * 256 + part * 256, 256)

        def scores(p, part):
            lanes = slice(p * 128, p * 128 + 128)
            s_buf[p % 2][:, part * 256:part * 256 + 256] = lax.dot_general(
                q2[p, rows_at(b * 256, 256), :], k[keys(part), lanes], NT, preferred_element_type=F32)

        for part in range(3):
            scores(0, part)
        for u in range(9):
            o = None
            for part in range(3):
                if u + 1 < 8:
                    scores(u + 1, part)
                if u > 0:
                    lanes = slice((u - 1) * 128, u * 128)
                    term = jnp.dot(p_buf[(u - 1) % 2][:, part * 256:part * 256 + 256], v[keys(part), lanes],
                                   preferred_element_type=F32)
                    o = term if o is None else o + term
                if u < 8:
                    for r in ((0, 5), (5, 10), (10, 16))[part:part + 1]:
                        for c in range(*r):
                            soft_rows(s_buf[u % 2], near_bias, p_buf[u % 2], ml_buf[u % 2], c * 16, 16)
            if u > 0:
                mlb = ml_buf[(u - 1) % 2]
                near_o[qrows, lanes] = jnp.where(low, o[0:128], o[128:256])
                near_m[qrows, lanes] = jnp.where(low, mlb[0, 0:128], mlb[0, 128:256])
                near_l[qrows, lanes] = jnp.where(low, mlb[1, 0:128], mlb[1, 128:256])

    @pl.loop(0, 4)
    def _(t):
        @pl.when(t == 2)
        def _():
            pl.when(has_down)(go_up[0].wait_recv)
            pl.when(has_up)(go_down[0].wait_recv)
            when_all(has_left & has_down, [west_up.wait_recv])
            when_all(has_left & has_up, [west_down.wait_recv])
            when_all(has_right & has_down, [east_up.wait_recv])
            when_all(has_right & has_up, [east_down.wait_recv])

            @pl.loop(0, 4)
            def _(i):
                normed[rows_at(i * 128, 128), :] = norm_rows(
                    rim[i // 2 * 5, rows_at(lax.rem(i, 2) * 128, 128), :].astype(F32), gain[...], beta[...]).astype(BF16)
            ends = (0, 128, 1280, 1408)
            project(wk, 1024, k, ends)
            project(wv, 2048, v, ends)

        band_step(t)

        @pl.when(t == 0)
        def _():
            pl.loop(1, 16)(lambda d: stage2(d).wait())
            total = p2[ew]
            for d in range(1, 16):
                total = total + buf2[d]
            g[ew] = total
            pl.loop(1, 16)(lambda d: stage3(d).start())

        @pl.when(t == 1)
        def _():
            @pl.loop(1, 16)
            def _(d):
                stage3(d).wait_send()
                stage3_in(d).wait_recv()

            pooled = jnp.concatenate([g[:, i, :] for i in range(8)], axis=1)
            ctx[core, unit] = norm_rows(pooled, cgain[...], cbias[...]).astype(BF16)
            pl.loop(1, 16)(lambda d: stage4(d).start())

    @pl.loop(1, 16)
    def _(d):
        stage4(d).wait_send()
        stage4_in(d).wait_recv()

    for i in range(2):
        for j in range(8):
            at = i * 128 + j * 16
            normed[at:at + 16, :] = ctx[i, j]
    give = pltpu.make_async_copy(normed.at[pl.ds(0, 256)], ctx_out, load.at[0])
    give.start()

    for weight, bias_at, dst in ((wk, 1024, kc), (wv, 2048, vc)):
        @pl.loop(0, 4)
        def _(n):
            cols = rows_at(n * 256, 256)
            y = jnp.dot(normed[0:256, :], weight[:, cols], preferred_element_type=F32)
            dst[:, cols] = (y + wb[:, rows_at(bias_at + n * 256, 256)]).astype(BF16)

    @pl.loop(0, 8)
    def _(p):
        lanes = rows_at(p * 128, 128)
        for half in range(2):
            cs[half * 512:half * 512 + 512, :] = lax.dot_general(
                q2[p, half * 512:half * 512 + 512, :], kc[:, lanes], NT, preferred_element_type=F32)
        for c in range(32):
            soft_rows(cs, None, cp, cml, c * 32, 32)
        o = jnp.dot(cp[...], vc[:, lanes], preferred_element_type=F32)
        for b in range(4):
            a0, a1 = slice(b * 256, b * 256 + 128), slice(b * 256 + 128, b * 256 + 256)
            rows = slice(b * 128, b * 128 + 128)
            oc = jnp.where(low, o[a0], o[a1])
            mc = jnp.where(low, cml[0, a0, :], cml[0, a1, :])
            lc = jnp.where(low, cml[1, a0, :], cml[1, a1, :])
            mn = near_m[rows, lanes]
            m = jnp.maximum(mn, mc)
            fn, fc = jnp.exp(mn - m), jnp.exp(mc - m)
            both = near_o[rows, lanes] * fn + oc * fc
            att[rows, lanes] = (both / (near_l[rows, lanes] * fn + lc * fc)).astype(BF16)

    loads[5].wait()

    @pl.loop(0, 4)
    def _(n):
        cols = rows_at(n * 256, 256)
        y = jnp.dot(att[...], wo[:, cols], preferred_element_type=F32)
        out[:, cols] = (tokens[:, cols].astype(F32) + y + ob[:, cols]).astype(BF16)

    give.wait()
    when_all(has_left, [c.wait_send for c in go_left])
    when_all(has_right, [c.wait_send for c in go_right])
    when_all(has_up, [go_up[0].wait_send])
    when_all(has_down, [go_down[0].wait_send])
    when_all(has_left & has_up, [west_up.wait_send])
    when_all(has_left & has_down, [west_down.wait_send])
    when_all(has_right & has_up, [east_up.wait_send])
    when_all(has_right & has_down, [east_down.wait_send])


def on_device(tokens, norm_gain, norm_bias, projection_weight, projection_bias, context_gain, context_bias,
              output_weight, output_bias, context_positions):
    vm = pl.BlockSpec(memory_space=pltpu.VMEM)
    hbm = pl.BlockSpec(memory_space=pl.ANY)
    dma = pltpu.SemaphoreType.DMA

    def f32(*shape):
        return pltpu.VMEM(shape, F32)

    def b16(*shape):
        return pltpu.VMEM(shape, BF16)

    mixed, context = pl.pallas_call(
        layer,
        out_shape=(jax.ShapeDtypeStruct((512, 1024), BF16), jax.ShapeDtypeStruct((256, 1024), BF16)),
        in_specs=[hbm] * 4 + [vm] * 6,
        out_specs=(vm, hbm),
        scratch_shapes=[
            b16(512, 1024), pltpu.VMEM((64, 256), jnp.int32), b16(1024, 1024), b16(1024, 1024), b16(1024, 1024),
            b16(1024, 1024), b16(512, 1024), b16(1536, 1024), b16(1536, 1024), b16(8, 1024, 128), b16(512, 1024),
            f32(512, 1024), f32(512, 1024), f32(512, 1024), f32(128, 768),
            f32(256, 768), f32(256, 768), b16(256, 768), b16(256, 768), f32(2, 256, 128), f32(2, 256, 128),
            f32(1024, 256), b16(1024, 256), f32(2, 1024, 128), b16(256, 1024), b16(256, 1024), b16(2, 8, 16, 1024),
            b16(6, 256, 1024), b16(4, 64, 1024), b16(4, 64, 1024),
            b16(512, 256), f32(256, 1024), f32(128, 1024), f32(8, 16, 1024), f32(8, 16, 1024),
            f32(16, 8, 128), f32(16, 8, 128), f32(16, 8, 128),
            dma((6,)), dma((12,)), dma((12,)), dma, dma, dma((8,)), dma((8,)),
            dma((16,)), dma((16,)), dma((16,)), dma((16,)), dma((16,)), dma((16,)),
        ],
        compiler_params=pltpu.CompilerParams(collective_id=0, has_side_effects=True, vmem_limit_bytes=60 * 2**20),
        name="layer",
    )(tokens.reshape(512, 1024), context_positions.T, projection_weight, output_weight,
      norm_gain.reshape(1, -1), norm_bias.reshape(1, -1), projection_bias.reshape(1, -1),
      context_gain.reshape(1, -1), context_bias.reshape(1, -1), output_bias.reshape(1, -1))
    return mixed.reshape(32, 16, 1024), context


def solution(mesh):
    return jax.shard_map(
        on_device,
        mesh=mesh,
        in_specs=(P("ns", "ew", None), P(), P(), P(), P(), P(), P(), P(), P(), P()),
        out_specs=(P("ns", "ew", None), P()),
        check_vma=False,
    )
```

```python
import jax
import jax.numpy as jnp
from jax import lax
from jax.experimental import pallas as pl
from jax.experimental.pallas import tpu as pltpu
from jax.sharding import PartitionSpec as P

F32 = jnp.float32
BF16 = jnp.bfloat16
MESH = pl.DeviceIdType.MESH
NT = (((1,), (1,)), ((), ()))
TN = (((0,), (0,)), ((), ()))


def rows_at(start, size):
    return pl.ds(pl.multiple_of(start, size), size)


def norm_rows(x, gain, bias):
    centre = x - jnp.mean(x, axis=-1, keepdims=True)
    spread = jnp.mean(centre * centre, axis=-1, keepdims=True)
    return centre * lax.rsqrt(spread + 1e-05) * gain + bias


def layer(tokens_hbm, pos_hbm, w_hbm, wo_hbm, gain_hbm, beta_hbm, wb_hbm, cgain_hbm, cbias_hbm, ob_hbm, out, ctx_out,
          gain, beta, wb, cgain, cbias, ob, pos, field, wall, normed, kvq, att, near_o, near_m, near_l, near_bias,
          s_a, s_b, p_a, p_b, ml_a, ml_b, cs, cp, cml, kvc, ctx,
          rim, send_l, send_r, counts, partial, buf0, p1, buf1, p2, buf2, g,
          load, halo_s, halo_r, s0, r0, s1, r1, s2, r2, s3, r3, s4, r4):
    ns = lax.axis_index("ns")
    ew = lax.axis_index("ew")
    core = lax.rem(ns, 2)
    unit = ns // 2

    barrier = pltpu.get_barrier_semaphore()

    @pl.loop(1, 16)
    def _(d):
        pl.semaphore_signal(barrier, inc=1, device_id=(lax.rem(ns + d, 16), ew), device_id_type=MESH)
        pl.semaphore_signal(barrier, inc=1, device_id=(ns, lax.rem(ew + d, 16)), device_id_type=MESH)

    moves = [(tokens_hbm.at[pl.ds(b * 128, 128)], rim.at[b + 1, pl.ds(0, 128)]) for b in range(4)]
    moves += [(pos_hbm, pos), (gain_hbm, gain), (beta_hbm, beta), (wb_hbm, wb), (cgain_hbm, cgain), (cbias_hbm, cbias),
              (ob_hbm, ob)]
    for t in range(6):
        moves.append((w_hbm.at[:, pl.ds((t * 512 + 1024) % 3072, 512)], wall.at[t]))
    for t in range(2):
        moves.append((wo_hbm.at[:, pl.ds(t * 512, 512)], wall.at[6 + t]))
    loads = [pltpu.make_async_copy(a, b, load.at[i]) for i, (a, b) in enumerate(moves)]
    for c in loads:
        c.start()
    for c in loads[:4]:
        c.wait()

    @pl.loop(0, 4)
    def _(b):
        x = rim[b + 1, 0:128, :].astype(F32).reshape(8, 2, 8, 1024)
        send_l[b] = x[:, 0].reshape(64, 1024).astype(BF16)
        send_r[b] = x[:, 1].reshape(64, 1024).astype(BF16)

    up, down, left, right = (ns - 1, ew), (ns + 1, ew), (ns, ew - 1), (ns, ew + 1)

    def halo(i, src, dst, device):
        return pltpu.make_async_remote_copy(src_ref=src, dst_ref=dst, send_sem=halo_s.at[i], recv_sem=halo_r.at[i],
                                            device_id=device, device_id_type=MESH)
    west, east = pl.ds(128, 64), pl.ds(192, 64)
    go_left = [halo(0, send_l.at[0], rim.at[1, east], left), halo(1, send_l.at[3], rim.at[4, east], left),
               halo(2, send_l.at[pl.ds(1, 2)], rim.at[pl.ds(2, 2), east], left)]
    go_right = [halo(3, send_r.at[0], rim.at[1, west], right), halo(4, send_r.at[3], rim.at[4, west], right),
                halo(5, send_r.at[pl.ds(1, 2)], rim.at[pl.ds(2, 2), west], right)]
    go_up = [halo(6, rim.at[1, pl.ds(0, 128)], rim.at[5, pl.ds(0, 128)], up)]
    go_down = [halo(7, rim.at[4, pl.ds(0, 128)], rim.at[0, pl.ds(0, 128)], down)]
    west_up = halo(8, rim.at[1, west], rim.at[5, west], up)
    west_down = halo(9, rim.at[4, west], rim.at[0, west], down)
    east_up = halo(10, rim.at[1, east], rim.at[5, east], up)
    east_down = halo(11, rim.at[4, east], rim.at[0, east], down)
    has_up, has_down, has_left, has_right = ns > 0, ns < 15, ew > 0, ew < 15

    def when_all(cond, calls):
        @pl.when(cond)
        def _():
            for c in calls:
                c()

    loads[4].wait()
    lr = (pos[...] >> 8) - ns * 32
    lc = (pos[...] & 255) - ew * 16
    own = (lr >= 0) & (lr < 32) & (lc >= 0) & (lc < 16)
    pos[...] = jnp.where(own, (lr & 7) * 16 + lc, -1)
    field[...] = jnp.where(own, lax.shift_left(jnp.ones_like(lr), (lr >> 3) * 8), 0)

    @pl.loop(0, 2)
    def _(t):
        ids = lax.broadcasted_iota(jnp.int32, (64, 256), 0) + t * 64
        total = jnp.zeros((64, 256), jnp.int32)
        for p in range(64):
            total = total + jnp.where(pos[p:p + 1, :] == ids, field[p:p + 1, :], 0)
        for i in range(4):
            part = (total >> (8 * i)) & 255
            counts[rows_at(i * 128 + t * 64, 64), :] = part.astype(F32).astype(BF16)

    pl.semaphore_wait(barrier, 30)
    for i in range(3):
        pl.when(has_left)(go_left[i].start)
        pl.when(has_right)(go_right[i].start)
    pl.when(has_up)(go_up[0].start)
    pl.when(has_down)(go_down[0].start)

    @pl.when(jnp.logical_not(has_up))
    def _():
        rim[0] = jnp.zeros((256, 1024), BF16)

    @pl.when(jnp.logical_not(has_down))
    def _():
        rim[5] = jnp.zeros((256, 1024), BF16)

    for gone, at in ((ew == 0, 128), (ew == 15, 192)):
        @pl.when(gone)
        def _():
            @pl.loop(0, 6)
            def _(t):
                rim[t, at:at + 64, :] = jnp.zeros((64, 1024), BF16)

    own_tokens = rim[1:5, 0:128, :].reshape(512, 1024)
    for t in range(2):
        cols = slice(t * 512, t * 512 + 512)
        partial[:, cols] = lax.dot_general(counts[...], own_tokens[:, cols], TN, preferred_element_type=F32)

    pair = pltpu.make_async_remote_copy(
        src_ref=partial.at[rows_at((1 - core) * 128, 128)], dst_ref=buf0, send_sem=s0, recv_sem=r0,
        device_id=(ns + 1 - 2 * core, ew), device_id_type=MESH)
    pair.start()

    def stage1(d):
        to = lax.rem(unit + d, 8)
        return pltpu.make_async_remote_copy(src_ref=p1.at[to], dst_ref=buf1.at[d], send_sem=s1.at[d], recv_sem=r1.at[d],
                                            device_id=(to * 2 + core, ew), device_id_type=MESH)
    def stage2(d):
        to = lax.rem(ew + d, 16)
        return pltpu.make_async_remote_copy(src_ref=p2.at[to], dst_ref=buf2.at[d], send_sem=s2.at[d], recv_sem=r2.at[d],
                                            device_id=(ns, to), device_id_type=MESH)
    def stage3(d):
        return pltpu.make_async_remote_copy(src_ref=g.at[ew], dst_ref=g.at[ew], send_sem=s3.at[d], recv_sem=r3.at[d],
                                            device_id=(ns, lax.rem(ew + d, 16)), device_id_type=MESH)

    def stage3_in(d):
        at = lax.rem(ew + 16 - d, 16)
        return pltpu.make_async_remote_copy(src_ref=g.at[at], dst_ref=g.at[at], send_sem=s3.at[d], recv_sem=r3.at[d],
                                            device_id=(ns, at), device_id_type=MESH)

    def stage4(d):
        mine = ctx.at[core, unit]
        return pltpu.make_async_remote_copy(src_ref=mine, dst_ref=mine, send_sem=s4.at[d], recv_sem=r4.at[d],
                                            device_id=(lax.rem(ns + d, 16), ew), device_id_type=MESH)

    def stage4_in(d):
        at = lax.rem(ns + 16 - d, 16)
        theirs = ctx.at[lax.rem(at, 2), at // 2]
        return pltpu.make_async_remote_copy(src_ref=theirs, dst_ref=theirs, send_sem=s4.at[d], recv_sem=r4.at[d],
                                            device_id=(at, ew), device_id_type=MESH)

    def start_stage1():
        pair.wait()

        @pl.loop(0, 8)
        def _(t):
            p1[t] = partial[rows_at(core * 128 + t * 16, 16), :] + buf0[rows_at(t * 16, 16), :]
        pl.loop(1, 8)(lambda d: stage1(d).start())

    def start_stage2():
        pl.loop(1, 8)(lambda d: stage1(d).wait())
        total = p1[unit]
        for d in range(1, 8):
            total = total + buf1[d]
        for i in range(8):
            p2[:, i, :] = total[:, i * 128:i * 128 + 128]
        pl.loop(1, 16)(lambda d: stage2(d).start())

    def start_stage3():
        pl.loop(1, 16)(lambda d: stage2(d).wait())
        total = p2[ew]
        for d in range(1, 16):
            total = total + buf2[d]
        g[ew] = total
        pl.loop(1, 16)(lambda d: stage3(d).start())

    def start_stage4():
        @pl.loop(1, 16)
        def _(d):
            stage3(d).wait_send()
            stage3_in(d).wait_recv()

        pooled = jnp.concatenate([g[:, i, :] for i in range(8)], axis=1)
        ctx[core, unit] = norm_rows(pooled, cgain[...], cbias[...]).astype(BF16)
        pl.loop(1, 16)(lambda d: stage4(d).start())

    low = lax.broadcasted_iota(jnp.int32, (128, 128), 1) < 64
    first = jnp.where(low, 0.125, 0.0).astype(BF16)
    second = jnp.where(low, 0.0, 0.125).astype(BF16)

    s_buf, p_buf, ml_buf = (s_a, s_b), (p_a, p_b), (ml_a, ml_b)

    def soft_rows(s, bias, pb, mlb, at, size):
        rows = slice(at, at + size)
        x = s[rows, :]
        if bias is not None:
            x = x + bias[at % 128:at % 128 + size, :]
        m = jnp.max(x, axis=1, keepdims=True)
        e = jnp.exp(x - m)
        l = jnp.sum(e, axis=1, keepdims=True)
        pb[rows, :] = e.astype(BF16)
        mlb[0, rows, :] = jnp.broadcast_to(m, (size, 128))
        mlb[1, rows, :] = jnp.broadcast_to(l, (size, 128))

    def band_step(b):
        for j in range(6):
            qi = lax.broadcasted_iota(jnp.int32, (128, 128), 0)
            ki = lax.broadcasted_iota(jnp.int32, (128, 128), 1)
            qr = 8 + qi // 16
            qc = 8 + qi % 16
            if j % 2 == 0:
                kr = 8 * (j // 2) + ki // 16
                kc_ = 8 + ki % 16
            else:
                kr = 8 * (j // 2) + (ki % 64) // 8
                kc_ = ki % 8 + jnp.where(ki < 64, 0, 24)
            gr = ns * 32 + 8 * b - 8 + kr
            gc = ew * 16 - 8 + kc_
            ok = ((kr - qr <= 7) & (qr - kr <= 7) & (kc_ - qc <= 7) & (qc - kc_ <= 7)
                  & (gr >= 0) & (gr < 512) & (gc >= 0) & (gc < 256))
            near_bias[:, j * 128:j * 128 + 128] = jnp.where(ok, 0.0, -1e30)

        qrows = rows_at(b * 128, 128)

        def keys(part):
            return rows_at(b * 256 + part * 256, 256)

        def scores(p, part):
            lanes = slice(p % 4 * 128, p % 4 * 128 + 128)
            q = kvq[4 + p // 4, rows_at(b * 256 + 256, 128), lanes]
            q = jnp.concatenate([q * first, q * second], axis=0)
            s_buf[p % 2][:, part * 256:part * 256 + 256] = lax.dot_general(
                q, kvq[p // 4, keys(part), lanes], NT, preferred_element_type=F32)

        for part in range(3):
            scores(0, part)
        for u in range(9):
            o = None
            for part in range(3):
                if u + 1 < 8:
                    scores(u + 1, part)
                if u > 0:
                    lanes = slice((u - 1) * 128, u * 128)
                    term = jnp.dot(p_buf[(u - 1) % 2][:, part * 256:part * 256 + 256], kvq[2 + (u - 1) // 4, keys(part), (u - 1) % 4 * 128:(u - 1) % 4 * 128 + 128],
                                   preferred_element_type=F32)
                    o = term if o is None else o + term
                if u < 8:
                    for r in ((0, 5), (5, 10), (10, 16))[part:part + 1]:
                        for c in range(*r):
                            soft_rows(s_buf[u % 2], near_bias, p_buf[u % 2], ml_buf[u % 2], c * 16, 16)
            if u > 0:
                mlb = ml_buf[(u - 1) % 2]
                near_o[qrows, lanes] = jnp.where(low, o[0:128], o[128:256])
                near_m[qrows, lanes] = jnp.where(low, mlb[0, 0:128], mlb[0, 128:256])
                near_l[qrows, lanes] = jnp.where(low, mlb[1, 0:128], mlb[1, 128:256])

    for c in loads[5:17]:
        c.wait()

    @pl.loop(0, 3)
    def _(phase):
        @pl.when(phase == 1)
        def _():
            for i in range(2):
                pl.when(has_left)(go_right[i].wait_recv)
                pl.when(has_right)(go_left[i].wait_recv)
            when_all(has_left & has_up, [west_up.start])
            when_all(has_left & has_down, [west_down.start])
            when_all(has_right & has_up, [east_up.start])
            when_all(has_right & has_down, [east_down.start])
            pl.when(has_left)(go_right[2].wait_recv)
            pl.when(has_right)(go_left[2].wait_recv)

        @pl.when(phase == 2)
        def _():
            start_stage4()
            pl.when(has_down)(go_up[0].wait_recv)
            pl.when(has_up)(go_down[0].wait_recv)
            when_all(has_left & has_down, [west_up.wait_recv])
            when_all(has_left & has_up, [west_down.wait_recv])
            when_all(has_right & has_down, [east_up.wait_recv])
            when_all(has_right & has_up, [east_down.wait_recv])

        ends = phase // 2
        blocks = [(1 - ends) * (2 * i + 2 + phase) + ends * (i // 2 * 10 + i % 2) for i in range(4)]
        groups = [(1 - ends) * (i + 1) + ends * (i // 2 * 5) for i in range(4)]
        sides = [(1 - ends) * phase + ends * (i % 2) for i in range(4)]
        for i in range(4):
            x = rim[groups[i], rows_at(sides[i] * 128, 128), :].astype(F32)
            normed[i * 128:i * 128 + 128, :] = norm_rows(x, gain[...], beta[...]).astype(BF16)

        @pl.loop(0, 4 + 2 * ((2 - phase) // 2))
        def _(t):
            pl.when((phase == 0) & (t == 2))(start_stage1)
            pl.when((phase == 1) & (t == 2))(start_stage2)
            y = jnp.dot(normed[...], wall[t], preferred_element_type=F32)
            y = (y + wb[:, rows_at(lax.rem(t * 512 + 1024, 3072), 512)]).astype(BF16)
            for i in range(4):
                kvq[t, rows_at(blocks[i] * 128, 128), :] = y[i * 128:i * 128 + 128]

        @pl.loop(0, 2 * ((phase + 1) // 2))
        def _(i):
            pl.when((phase == 1) & (i == 0))(start_stage3)
            band_step(lax.rem(2 * phase - 1 + i, 4))

    @pl.loop(1, 16)
    def _(d):
        stage4(d).wait_send()
        stage4_in(d).wait_recv()

    for i in range(2):
        for j in range(8):
            at = i * 128 + j * 16
            normed[at:at + 16, :] = ctx[i, j]
    ctx_out[...] = normed[0:256, :]

    @pl.loop(0, 4)
    def _(t):
        y = jnp.dot(normed[0:256, :], wall[t], preferred_element_type=F32)
        kvc[t] = (y + wb[:, rows_at(t * 512 + 1024, 512)]).astype(BF16)

    @pl.loop(0, 8)
    def _(p):
        lanes = rows_at(p * 128, 128)
        part = rows_at(lax.rem(p, 4) * 128, 128)
        qs = []
        for b in range(4):
            q = kvq[4 + p // 4, b * 256 + 256:b * 256 + 384, part]
            qs += [q * first, q * second]
        cs[...] = lax.dot_general(jnp.concatenate(qs, axis=0), kvc[p // 4, :, part], NT, preferred_element_type=F32)
        for c in range(32):
            soft_rows(cs, None, cp, cml, c * 32, 32)
        o = jnp.dot(cp[...], kvc[2 + p // 4, :, part], preferred_element_type=F32)
        for b in range(4):
            a0, a1 = slice(b * 256, b * 256 + 128), slice(b * 256 + 128, b * 256 + 256)
            rows = slice(b * 128, b * 128 + 128)
            oc = jnp.where(low, o[a0], o[a1])
            mc = jnp.where(low, cml[0, a0, :], cml[0, a1, :])
            lc = jnp.where(low, cml[1, a0, :], cml[1, a1, :])
            mn = near_m[rows, lanes]
            m = jnp.maximum(mn, mc)
            fn, fc = jnp.exp(mn - m), jnp.exp(mc - m)
            both = near_o[rows, lanes] * fn + oc * fc
            att[rows, lanes] = (both / (near_l[rows, lanes] * fn + lc * fc)).astype(BF16)

    for c in loads[17:]:
        c.wait()
    for n in range(2):
        cols = slice(n * 512, n * 512 + 512)
        y = jnp.dot(att[...], wall[6 + n], preferred_element_type=F32)
        for b in range(4):
            rows = slice(b * 128, b * 128 + 128)
            out[rows, cols] = (rim[b + 1, 0:128, cols].astype(F32) + y[rows] + ob[:, cols]).astype(BF16)

    when_all(has_left, [c.wait_send for c in go_left])
    when_all(has_right, [c.wait_send for c in go_right])
    when_all(has_up, [go_up[0].wait_send])
    when_all(has_down, [go_down[0].wait_send])
    when_all(has_left & has_up, [west_up.wait_send])
    when_all(has_left & has_down, [west_down.wait_send])
    when_all(has_right & has_up, [east_up.wait_send])
    when_all(has_right & has_down, [east_down.wait_send])


def on_device(tokens, norm_gain, norm_bias, projection_weight, projection_bias, context_gain, context_bias,
              output_weight, output_bias, context_positions):
    vm = pl.BlockSpec(memory_space=pltpu.VMEM)
    hbm = pl.BlockSpec(memory_space=pltpu.MemorySpace.HBM)
    dma = pltpu.SemaphoreType.DMA

    def f32(*shape):
        return pltpu.VMEM(shape, F32)

    def b16(*shape):
        return pltpu.VMEM(shape, BF16)

    mixed, context = pl.pallas_call(
        layer,
        out_shape=(jax.ShapeDtypeStruct((512, 1024), BF16), jax.ShapeDtypeStruct((256, 1024), BF16)),
        in_specs=[hbm] * 10,
        out_specs=(vm, vm),
        scratch_shapes=[
            f32(1, 1024), f32(1, 1024), f32(1, 3072), f32(1, 1024), f32(1, 1024), f32(1, 1024),
            pltpu.VMEM((64, 256), jnp.int32), pltpu.VMEM((64, 256), jnp.int32), b16(8, 1024, 512), b16(512, 1024),
            b16(6, 1536, 512), b16(512, 1024),
            f32(512, 1024), f32(512, 1024), f32(512, 1024), f32(128, 768),
            f32(256, 768), f32(256, 768), b16(256, 768), b16(256, 768), f32(2, 256, 128), f32(2, 256, 128),
            f32(1024, 256), b16(1024, 256), f32(2, 1024, 128), b16(4, 256, 512), b16(2, 8, 16, 1024),
            b16(6, 256, 1024), b16(4, 64, 1024), b16(4, 64, 1024),
            b16(512, 256), f32(256, 1024), f32(128, 1024), f32(8, 16, 1024), f32(8, 16, 1024),
            f32(16, 8, 128), f32(16, 8, 128), f32(16, 8, 128),
            dma((19,)), dma((12,)), dma((12,)), dma, dma, dma((8,)), dma((8,)),
            dma((16,)), dma((16,)), dma((16,)), dma((16,)), dma((16,)), dma((16,)),
        ],
        compiler_params=pltpu.CompilerParams(collective_id=0, has_side_effects=True, vmem_limit_bytes=50 * 2**20),
        name="layer",
    )(*[pltpu.with_memory_space_constraint(a, pltpu.MemorySpace.HBM) for a in (
        tokens.reshape(512, 1024), context_positions.T, projection_weight, output_weight,
        norm_gain.reshape(1, -1), norm_bias.reshape(1, -1), projection_bias.reshape(1, -1),
        context_gain.reshape(1, -1), context_bias.reshape(1, -1), output_bias.reshape(1, -1))])
    return mixed.reshape(32, 16, 1024), context


def solution(mesh):
    return jax.shard_map(
        on_device,
        mesh=mesh,
        in_specs=(P("ns", "ew", None), P(), P(), P(), P(), P(), P(), P(), P(), P()),
        out_specs=(P("ns", "ew", None), P()),
        check_vma=False,
    )
```

```python
import jax
import jax.numpy as jnp
from jax import lax
from jax.experimental import pallas as pl
from jax.experimental.pallas import tpu as pltpu
from jax.sharding import PartitionSpec as P

F32 = jnp.float32
BF16 = jnp.bfloat16
MESH = pl.DeviceIdType.MESH
NT = (((1,), (1,)), ((), ()))
TN = (((0,), (0,)), ((), ()))


def rows_at(start, size):
    return pl.ds(pl.multiple_of(start, size), size)


def norm_rows(x, gain, bias):
    centre = x - jnp.mean(x, axis=-1, keepdims=True)
    spread = jnp.mean(centre * centre, axis=-1, keepdims=True)
    return centre * lax.rsqrt(spread + 1e-05) * gain + bias


def layer(tokens_hbm, pos_hbm, w_hbm, wo_hbm, gain_hbm, beta_hbm, wb_hbm, cgain_hbm, cbias_hbm, ob_hbm, out, ctx_out,
          gain, beta, wb, cgain, cbias, ob, tokens, pos, field, wq, wk, wv, wo, normed, k, v, q2, att, near_o, near_m, near_l, near_bias,
          s_a, s_b, p_a, p_b, ml_a, ml_b, cs, cp, cml, cs2, cp2, cml2, kc, vc, ctx,
          rim, send_l, send_r, counts, partial, buf0, p1, buf1, p2, buf2, g,
          load, halo_s, halo_r, s0, r0, s1, r1, s2, r2, s3, r3, s4, r4):
    ns = lax.axis_index("ns")
    ew = lax.axis_index("ew")
    core = lax.rem(ns, 2)
    unit = ns // 2

    barrier = pltpu.get_barrier_semaphore()

    @pl.loop(1, 16)
    def _(d):
        pl.semaphore_signal(barrier, inc=1, device_id=(lax.rem(ns + d, 16), ew), device_id_type=MESH)
        pl.semaphore_signal(barrier, inc=1, device_id=(ns, lax.rem(ew + d, 16)), device_id_type=MESH)

    loads = [pltpu.make_async_copy(a, b, load.at[i]) for i, (a, b) in enumerate((
        (tokens_hbm, tokens), (pos_hbm, pos), (w_hbm.at[:, pl.ds(1024, 1024)], wk), (w_hbm.at[:, pl.ds(2048, 1024)], wv),
        (w_hbm.at[:, pl.ds(0, 1024)], wq), (wo_hbm, wo), (gain_hbm, gain), (beta_hbm, beta), (wb_hbm, wb),
        (cgain_hbm, cgain), (cbias_hbm, cbias), (ob_hbm, ob)))]
    for c in loads[:2] + loads[6:] + loads[2:6]:
        c.start()
    loads[0].wait()

    @pl.loop(0, 4)
    def _(b):
        x = tokens[rows_at(b * 128, 128), :].astype(F32).reshape(8, 2, 8, 1024)
        send_l[b] = x[:, 0].reshape(64, 1024).astype(BF16)
        send_r[b] = x[:, 1].reshape(64, 1024).astype(BF16)

    up, down, left, right = (ns - 1, ew), (ns + 1, ew), (ns, ew - 1), (ns, ew + 1)

    def halo(i, src, dst, device):
        return pltpu.make_async_remote_copy(src_ref=src, dst_ref=dst, send_sem=halo_s.at[i], recv_sem=halo_r.at[i],
                                            device_id=device, device_id_type=MESH)
    west, east = pl.ds(128, 64), pl.ds(192, 64)
    go_left = [halo(0, send_l.at[0], rim.at[1, east], left), halo(1, send_l.at[3], rim.at[4, east], left),
               halo(2, send_l.at[pl.ds(1, 2)], rim.at[pl.ds(2, 2), east], left)]
    go_right = [halo(3, send_r.at[0], rim.at[1, west], right), halo(4, send_r.at[3], rim.at[4, west], right),
                halo(5, send_r.at[pl.ds(1, 2)], rim.at[pl.ds(2, 2), west], right)]
    go_up = [halo(6, tokens.at[pl.ds(0, 128)], rim.at[5, pl.ds(0, 128)], up)]
    go_down = [halo(7, tokens.at[pl.ds(384, 128)], rim.at[0, pl.ds(0, 128)], down)]
    west_up = halo(8, rim.at[1, west], rim.at[5, west], up)
    west_down = halo(9, rim.at[4, west], rim.at[0, west], down)
    east_up = halo(10, rim.at[1, east], rim.at[5, east], up)
    east_down = halo(11, rim.at[4, east], rim.at[0, east], down)
    has_up, has_down, has_left, has_right = ns > 0, ns < 15, ew > 0, ew < 15

    def when_all(cond, calls):
        @pl.when(cond)
        def _():
            for c in calls:
                c()

    pl.semaphore_wait(barrier, 30)
    for i in range(3):
        pl.when(has_left)(go_left[i].start)
        pl.when(has_right)(go_right[i].start)
    pl.when(has_up)(go_up[0].start)
    pl.when(has_down)(go_down[0].start)

    @pl.when(jnp.logical_not(has_up))
    def _():
        rim[0] = jnp.zeros((256, 1024), BF16)

    @pl.when(jnp.logical_not(has_down))
    def _():
        rim[5] = jnp.zeros((256, 1024), BF16)

    for gone, at in ((ew == 0, 128), (ew == 15, 192)):
        @pl.when(gone)
        def _():
            @pl.loop(0, 6)
            def _(t):
                rim[t, at:at + 64, :] = jnp.zeros((64, 1024), BF16)

    loads[1].wait()
    lr = (pos[...] >> 8) - ns * 32
    lc = (pos[...] & 255) - ew * 16
    own = (lr >= 0) & (lr < 32) & (lc >= 0) & (lc < 16)
    pos[...] = jnp.where(own, (lr & 7) * 16 + lc, -1)
    field[...] = jnp.where(own, lax.shift_left(jnp.ones_like(lr), (lr >> 3) * 8), 0)

    @pl.loop(0, 2)
    def _(t):
        ids = lax.broadcasted_iota(jnp.int32, (64, 256), 0) + t * 64
        total = jnp.zeros((64, 256), jnp.int32)
        for p in range(64):
            total = total + jnp.where(pos[p:p + 1, :] == ids, field[p:p + 1, :], 0)
        for i in range(4):
            part = (total >> (8 * i)) & 255
            counts[rows_at(i * 128 + t * 64, 64), :] = part.astype(F32).astype(BF16)

    for t in range(2):
        cols = slice(t * 512, t * 512 + 512)
        partial[:, cols] = lax.dot_general(counts[...], tokens[:, cols], TN, preferred_element_type=F32)

    pair = pltpu.make_async_remote_copy(
        src_ref=partial.at[rows_at((1 - core) * 128, 128)], dst_ref=buf0, send_sem=s0, recv_sem=r0,
        device_id=(ns + 1 - 2 * core, ew), device_id_type=MESH)
    pair.start()

    def project(weight, bias_at, dst, place):
        size = 128 * len(place)
        for n in range(2):
            cols = slice(n * 512, n * 512 + 512)
            y = jnp.dot(normed[0:size, :], weight[:, cols], preferred_element_type=F32)
            y = (y + wb[:, bias_at + n * 512:bias_at + n * 512 + 512]).astype(BF16)
            for i, at in enumerate(place):
                dst[at:at + 128, cols] = y[i * 128:i * 128 + 128]

    def norm_into(at, x):
        normed[at:at + x.shape[0], :] = norm_rows(x.astype(F32), gain[...], beta[...]).astype(BF16)

    for c in loads[6:]:
        c.wait()
    for i in range(2):
        norm_into(i * 256, tokens[i * 256:i * 256 + 256, :])

    mid_own = (256, 512, 768, 1024)
    mid_side = (384, 640, 896, 1152)
    loads[2].wait()
    project(wk, 1024, k, mid_own)
    pair.wait()

    @pl.loop(0, 8)
    def _(t):
        p1[t] = partial[rows_at(core * 128 + t * 16, 16), :] + buf0[rows_at(t * 16, 16), :]

    def stage1(d):
        to = lax.rem(unit + d, 8)
        return pltpu.make_async_remote_copy(src_ref=p1.at[to], dst_ref=buf1.at[d], send_sem=s1.at[d], recv_sem=r1.at[d],
                                            device_id=(to * 2 + core, ew), device_id_type=MESH)
    pl.loop(1, 8)(lambda d: stage1(d).start())

    loads[3].wait()
    project(wv, 2048, v, mid_own)

    low = lax.broadcasted_iota(jnp.int32, (128, 128), 1) < 64
    loads[4].wait()

    for n in range(2):
        cols = slice(n * 512, n * 512 + 512)
        y = jnp.dot(normed[...], wq[:, cols], preferred_element_type=F32)
        y = (y + wb[:, cols]).astype(BF16).astype(F32) * 0.125
        for b in range(4):
            for i in range(4):
                q = y[b * 128:b * 128 + 128, i * 128:i * 128 + 128]
                q2[n * 4 + i, b * 256:b * 256 + 128, :] = jnp.where(low, q, 0.0).astype(BF16)
                q2[n * 4 + i, b * 256 + 128:b * 256 + 256, :] = jnp.where(low, 0.0, q).astype(BF16)

    pl.when(has_down)(go_up[0].wait_recv)
    pl.when(has_up)(go_down[0].wait_recv)
    norm_into(0, rim[0, 0:128, :])
    norm_into(128, rim[5, 0:128, :])
    project(wk, 1024, k, (0, 1280))
    project(wv, 2048, v, (0, 1280))

    for i in range(2):
        pl.when(has_left)(go_right[i].wait_recv)
        pl.when(has_right)(go_left[i].wait_recv)
    when_all(has_left & has_up, [west_up.start])
    when_all(has_left & has_down, [west_down.start])
    when_all(has_right & has_up, [east_up.start])
    when_all(has_right & has_down, [east_down.start])
    pl.when(has_left)(go_right[2].wait_recv)
    pl.when(has_right)(go_left[2].wait_recv)

    pl.loop(1, 8)(lambda d: stage1(d).wait())
    total = p1[unit]
    for d in range(1, 8):
        total = total + buf1[d]
    for i in range(8):
        p2[:, i, :] = total[:, i * 128:i * 128 + 128]

    def stage2(d):
        to = lax.rem(ew + d, 16)
        return pltpu.make_async_remote_copy(src_ref=p2.at[to], dst_ref=buf2.at[d], send_sem=s2.at[d], recv_sem=r2.at[d],
                                            device_id=(ns, to), device_id_type=MESH)
    pl.loop(1, 16)(lambda d: stage2(d).start())

    for i in range(4):
        norm_into(i * 128, rim[i + 1, 128:256, :])
    project(wk, 1024, k, mid_side)
    project(wv, 2048, v, mid_side)

    def stage3(d):
        return pltpu.make_async_remote_copy(src_ref=g.at[ew], dst_ref=g.at[ew], send_sem=s3.at[d], recv_sem=r3.at[d],
                                            device_id=(ns, lax.rem(ew + d, 16)), device_id_type=MESH)

    def stage3_in(d):
        at = lax.rem(ew + 16 - d, 16)
        return pltpu.make_async_remote_copy(src_ref=g.at[at], dst_ref=g.at[at], send_sem=s3.at[d], recv_sem=r3.at[d],
                                            device_id=(ns, at), device_id_type=MESH)

    def stage4(d):
        mine = ctx.at[core, unit]
        return pltpu.make_async_remote_copy(src_ref=mine, dst_ref=mine, send_sem=s4.at[d], recv_sem=r4.at[d],
                                            device_id=(lax.rem(ns + d, 16), ew), device_id_type=MESH)

    def stage4_in(d):
        at = lax.rem(ns + 16 - d, 16)
        theirs = ctx.at[lax.rem(at, 2), at // 2]
        return pltpu.make_async_remote_copy(src_ref=theirs, dst_ref=theirs, send_sem=s4.at[d], recv_sem=r4.at[d],
                                            device_id=(at, ew), device_id_type=MESH)

    s_buf, p_buf, ml_buf = (s_a, s_b), (p_a, p_b), (ml_a, ml_b)

    def soft_rows(s, bias, pb, mlb, at, size):
        rows = slice(at, at + size)
        x = s[rows, :]
        if bias is not None:
            x = x + bias[at % 128:at % 128 + size, :]
        m = jnp.max(x, axis=1, keepdims=True)
        e = jnp.exp(x - m)
        l = jnp.sum(e, axis=1, keepdims=True)
        pb[rows, :] = e.astype(BF16)
        mlb[0, rows, :] = jnp.broadcast_to(m, (size, 128))
        mlb[1, rows, :] = jnp.broadcast_to(l, (size, 128))

    def band_step(t):
        b = lax.rem(t + 1, 4)
        for j in range(6):
            qi = lax.broadcasted_iota(jnp.int32, (128, 128), 0)
            ki = lax.broadcasted_iota(jnp.int32, (128, 128), 1)
            qr = 8 + qi // 16
            qc = 8 + qi % 16
            if j % 2 == 0:
                kr = 8 * (j // 2) + ki // 16
                kc_ = 8 + ki % 16
            else:
                kr = 8 * (j // 2) + (ki % 64) // 8
                kc_ = ki % 8 + jnp.where(ki < 64, 0, 24)
            gr = ns * 32 + 8 * b - 8 + kr
            gc = ew * 16 - 8 + kc_
            ok = ((kr - qr <= 7) & (qr - kr <= 7) & (kc_ - qc <= 7) & (qc - kc_ <= 7)
                  & (gr >= 0) & (gr < 512) & (gc >= 0) & (gc < 256))
            near_bias[:, j * 128:j * 128 + 128] = jnp.where(ok, 0.0, -1e30)

        qrows = rows_at(b * 128, 128)

        def keys(part):
            return rows_at(b * 256 + part * 256, 256)

        def scores(p, part):
            lanes = slice(p * 128, p * 128 + 128)
            s_buf[p % 2][:, part * 256:part * 256 + 256] = lax.dot_general(
                q2[p, rows_at(b * 256, 256), :], k[keys(part), lanes], NT, preferred_element_type=F32)

        for part in range(3):
            scores(0, part)
        for u in range(9):
            o = None
            for part in range(3):
                if u + 1 < 8:
                    scores(u + 1, part)
                if u > 0:
                    lanes = slice((u - 1) * 128, u * 128)
                    term = jnp.dot(p_buf[(u - 1) % 2][:, part * 256:part * 256 + 256], v[keys(part), lanes],
                                   preferred_element_type=F32)
                    o = term if o is None else o + term
                if u < 8:
                    for r in ((0, 5), (5, 10), (10, 16))[part:part + 1]:
                        for c in range(*r):
                            soft_rows(s_buf[u % 2], near_bias, p_buf[u % 2], ml_buf[u % 2], c * 16, 16)
            if u > 0:
                mlb = ml_buf[(u - 1) % 2]
                near_o[qrows, lanes] = jnp.where(low, o[0:128], o[128:256])
                near_m[qrows, lanes] = jnp.where(low, mlb[0, 0:128], mlb[0, 128:256])
                near_l[qrows, lanes] = jnp.where(low, mlb[1, 0:128], mlb[1, 128:256])

    pl.loop(1, 16)(lambda d: stage2(d).wait())
    total = p2[ew]
    for d in range(1, 16):
        total = total + buf2[d]
    g[ew] = total
    pl.loop(1, 16)(lambda d: stage3(d).start())

    @pl.loop(0, 4)
    def _(t):
        @pl.when(t == 2)
        def _():
            when_all(has_left & has_down, [west_up.wait_recv])
            when_all(has_left & has_up, [west_down.wait_recv])
            when_all(has_right & has_down, [east_up.wait_recv])
            when_all(has_right & has_up, [east_down.wait_recv])

            norm_into(0, rim[0, 128:256, :])
            norm_into(128, rim[5, 128:256, :])
            project(wk, 1024, k, (128, 1408))
            project(wv, 2048, v, (128, 1408))

        band_step(t)

        @pl.when(t == 1)
        def _():
            @pl.loop(1, 16)
            def _(d):
                stage3(d).wait_send()
                stage3_in(d).wait_recv()

            pooled = jnp.concatenate([g[:, i, :] for i in range(8)], axis=1)
            ctx[core, unit] = norm_rows(pooled, cgain[...], cbias[...]).astype(BF16)
            pl.loop(1, 16)(lambda d: stage4(d).start())

    @pl.loop(1, 16)
    def _(d):
        stage4(d).wait_send()
        stage4_in(d).wait_recv()

    for i in range(2):
        for j in range(8):
            at = i * 128 + j * 16
            normed[at:at + 16, :] = ctx[i, j]
    ctx_out[...] = normed[0:256, :]

    project(wk, 1024, kc, (0, 128))
    project(wv, 2048, vc, (0, 128))

    def context_pair(p, cs, cp, cml):
        lanes = rows_at(p * 128, 128)
        for half in range(2):
            cs[half * 512:half * 512 + 512, :] = lax.dot_general(
                q2[p, half * 512:half * 512 + 512, :], kc[:, lanes], NT, preferred_element_type=F32)
        for c in range(32):
            soft_rows(cs, None, cp, cml, c * 32, 32)
        o = jnp.dot(cp[...], vc[:, lanes], preferred_element_type=F32)
        for b in range(4):
            a0, a1 = slice(b * 256, b * 256 + 128), slice(b * 256 + 128, b * 256 + 256)
            rows = slice(b * 128, b * 128 + 128)
            oc = jnp.where(low, o[a0], o[a1])
            mc = jnp.where(low, cml[0, a0, :], cml[0, a1, :])
            lc = jnp.where(low, cml[1, a0, :], cml[1, a1, :])
            mn = near_m[rows, lanes]
            m = jnp.maximum(mn, mc)
            fn, fc = jnp.exp(mn - m), jnp.exp(mc - m)
            both = near_o[rows, lanes] * fn + oc * fc
            att[rows, lanes] = (both / (near_l[rows, lanes] * fn + lc * fc)).astype(BF16)

    @pl.loop(0, 4)
    def _(i):
        context_pair(i * 2, cs, cp, cml)
        context_pair(i * 2 + 1, cs2, cp2, cml2)

    loads[5].wait()

    for n in range(2):
        cols = slice(n * 512, n * 512 + 512)
        y = jnp.dot(att[...], wo[:, cols], preferred_element_type=F32)
        out[:, cols] = (tokens[:, cols].astype(F32) + y + ob[:, cols]).astype(BF16)

    when_all(has_left, [c.wait_send for c in go_left])
    when_all(has_right, [c.wait_send for c in go_right])
    when_all(has_up, [go_up[0].wait_send])
    when_all(has_down, [go_down[0].wait_send])
    when_all(has_left & has_up, [west_up.wait_send])
    when_all(has_left & has_down, [west_down.wait_send])
    when_all(has_right & has_up, [east_up.wait_send])
    when_all(has_right & has_down, [east_down.wait_send])


def on_device(tokens, norm_gain, norm_bias, projection_weight, projection_bias, context_gain, context_bias,
              output_weight, output_bias, context_positions):
    vm = pl.BlockSpec(memory_space=pltpu.VMEM)
    hbm = pl.BlockSpec(memory_space=pltpu.MemorySpace.HBM)
    dma = pltpu.SemaphoreType.DMA

    def f32(*shape):
        return pltpu.VMEM(shape, F32)

    def b16(*shape):
        return pltpu.VMEM(shape, BF16)

    mixed, context = pl.pallas_call(
        layer,
        out_shape=(jax.ShapeDtypeStruct((512, 1024), BF16), jax.ShapeDtypeStruct((256, 1024), BF16)),
        in_specs=[hbm] * 10,
        out_specs=(vm, vm),
        scratch_shapes=[
            f32(1, 1024), f32(1, 1024), f32(1, 3072), f32(1, 1024), f32(1, 1024), f32(1, 1024),
            b16(512, 1024), pltpu.VMEM((64, 256), jnp.int32), pltpu.VMEM((64, 256), jnp.int32), b16(1024, 1024), b16(1024, 1024), b16(1024, 1024),
            b16(1024, 1024), b16(512, 1024), b16(1536, 1024), b16(1536, 1024), b16(8, 1024, 128), b16(512, 1024),
            f32(512, 1024), f32(512, 1024), f32(512, 1024), f32(128, 768),
            f32(256, 768), f32(256, 768), b16(256, 768), b16(256, 768), f32(2, 256, 128), f32(2, 256, 128),
            f32(1024, 256), b16(1024, 256), f32(2, 1024, 128), f32(1024, 256), b16(1024, 256), f32(2, 1024, 128), b16(256, 1024), b16(256, 1024), b16(2, 8, 16, 1024),
            b16(6, 256, 1024), b16(4, 64, 1024), b16(4, 64, 1024),
            b16(512, 256), f32(256, 1024), f32(128, 1024), f32(8, 16, 1024), f32(8, 16, 1024),
            f32(16, 8, 128), f32(16, 8, 128), f32(16, 8, 128),
            dma((12,)), dma((12,)), dma((12,)), dma, dma, dma((8,)), dma((8,)),
            dma((16,)), dma((16,)), dma((16,)), dma((16,)), dma((16,)), dma((16,)),
        ],
        compiler_params=pltpu.CompilerParams(collective_id=0, has_side_effects=True, vmem_limit_bytes=54 * 2**20),
        name="layer",
    )(*[pltpu.with_memory_space_constraint(a, pltpu.MemorySpace.HBM) for a in (
        tokens.reshape(512, 1024), context_positions.T, projection_weight, output_weight,
        norm_gain.reshape(1, -1), norm_bias.reshape(1, -1), projection_bias.reshape(1, -1),
        context_gain.reshape(1, -1), context_bias.reshape(1, -1), output_bias.reshape(1, -1))])
    return mixed.reshape(32, 16, 1024), context


def solution(mesh):
    return jax.shard_map(
        on_device,
        mesh=mesh,
        in_specs=(P("ns", "ew", None), P(), P(), P(), P(), P(), P(), P(), P(), P()),
        out_specs=(P("ns", "ew", None), P()),
        check_vma=False,
    )
```

```python
import jax
import jax.numpy as jnp
from jax import lax
from jax.experimental import pallas as pl
from jax.experimental.pallas import tpu as pltpu
from jax.sharding import PartitionSpec as P

F32 = jnp.float32
BF16 = jnp.bfloat16
MESH = pl.DeviceIdType.MESH
NT = (((1,), (1,)), ((), ()))
TN = (((0,), (0,)), ((), ()))


def rows_at(start, size):
    return pl.ds(pl.multiple_of(start, size), size)


def norm_rows(x, gain, bias):
    centre = x - jnp.mean(x, axis=-1, keepdims=True)
    spread = jnp.mean(centre * centre, axis=-1, keepdims=True)
    return centre * lax.rsqrt(spread + 1e-05) * gain + bias


def layer(tokens_hbm, pos_hbm, w_hbm, wo_hbm, gain_hbm, beta_hbm, wb_hbm, cgain_hbm, cbias_hbm, ob_hbm, out, ctx_out,
          gain, beta, wb, cgain, cbias, ob, tokens, pos, field, wq, wk, wv, wo, normed, k, v, q2, att, near_o, near_m, near_l, near_bias,
          s_a, s_b, p_a, p_b, ml_a, ml_b, cs, cp, cml, cs2, cp2, cml2, kc, vc, ctx,
          rim, send_l, send_r, counts, partial, buf0, p1, buf1, p2, buf2, g,
          load, halo_s, halo_r, s0, r0, s1, r1, s2, r2, s3, r3, s4, r4):
    ns = lax.axis_index("ns")
    ew = lax.axis_index("ew")
    core = lax.rem(ns, 2)
    unit = ns // 2

    barrier = pltpu.get_barrier_semaphore()

    @pl.loop(1, 16)
    def _(d):
        pl.semaphore_signal(barrier, inc=1, device_id=(lax.rem(ns + d, 16), ew), device_id_type=MESH)
        pl.semaphore_signal(barrier, inc=1, device_id=(ns, lax.rem(ew + d, 16)), device_id_type=MESH)

    loads = [pltpu.make_async_copy(a, b, load.at[i]) for i, (a, b) in enumerate((
        (tokens_hbm, tokens), (pos_hbm, pos), (w_hbm.at[:, pl.ds(1024, 1024)], wk), (w_hbm.at[:, pl.ds(2048, 1024)], wv),
        (w_hbm.at[:, pl.ds(0, 1024)], wq), (wo_hbm, wo), (gain_hbm, gain), (beta_hbm, beta), (wb_hbm, wb),
        (cgain_hbm, cgain), (cbias_hbm, cbias), (ob_hbm, ob)))]
    for c in loads[:2] + loads[6:] + loads[2:6]:
        c.start()
    loads[0].wait()

    @pl.loop(0, 4)
    def _(b):
        x = tokens[rows_at(b * 128, 128), :].astype(F32).reshape(8, 2, 8, 1024)
        send_l[b] = x[:, 0].reshape(64, 1024).astype(BF16)
        send_r[b] = x[:, 1].reshape(64, 1024).astype(BF16)

    up, down, left, right = (ns - 1, ew), (ns + 1, ew), (ns, ew - 1), (ns, ew + 1)

    def halo(i, src, dst, device):
        return pltpu.make_async_remote_copy(src_ref=src, dst_ref=dst, send_sem=halo_s.at[i], recv_sem=halo_r.at[i],
                                            device_id=device, device_id_type=MESH)
    west, east = pl.ds(128, 64), pl.ds(192, 64)
    go_left = [halo(0, send_l.at[0], rim.at[1, east], left), halo(1, send_l.at[3], rim.at[4, east], left),
               halo(2, send_l.at[pl.ds(1, 2)], rim.at[pl.ds(2, 2), east], left)]
    go_right = [halo(3, send_r.at[0], rim.at[1, west], right), halo(4, send_r.at[3], rim.at[4, west], right),
                halo(5, send_r.at[pl.ds(1, 2)], rim.at[pl.ds(2, 2), west], right)]
    go_up = [halo(6, tokens.at[pl.ds(0, 128)], rim.at[5, pl.ds(0, 128)], up)]
    go_down = [halo(7, tokens.at[pl.ds(384, 128)], rim.at[0, pl.ds(0, 128)], down)]
    west_up = halo(8, rim.at[1, west], rim.at[5, west], up)
    west_down = halo(9, rim.at[4, west], rim.at[0, west], down)
    east_up = halo(10, rim.at[1, east], rim.at[5, east], up)
    east_down = halo(11, rim.at[4, east], rim.at[0, east], down)
    has_up, has_down, has_left, has_right = ns > 0, ns < 15, ew > 0, ew < 15

    def when_all(cond, calls):
        @pl.when(cond)
        def _():
            for c in calls:
                c()

    pl.semaphore_wait(barrier, 30)
    for i in range(3):
        pl.when(has_left)(go_left[i].start)
        pl.when(has_right)(go_right[i].start)
    pl.when(has_up)(go_up[0].start)
    pl.when(has_down)(go_down[0].start)

    @pl.when(jnp.logical_not(has_up))
    def _():
        rim[0] = jnp.zeros((256, 1024), BF16)

    @pl.when(jnp.logical_not(has_down))
    def _():
        rim[5] = jnp.zeros((256, 1024), BF16)

    for gone, at in ((ew == 0, 128), (ew == 15, 192)):
        @pl.when(gone)
        def _():
            @pl.loop(0, 6)
            def _(t):
                rim[t, at:at + 64, :] = jnp.zeros((64, 1024), BF16)

    loads[1].wait()
    lr = (pos[...] >> 8) - ns * 32
    lc = (pos[...] & 255) - ew * 16
    own = (lr >= 0) & (lr < 32) & (lc >= 0) & (lc < 16)
    pos[...] = jnp.where(own, (lr & 7) * 16 + lc, -1)
    field[...] = jnp.where(own, lax.shift_left(jnp.ones_like(lr), (lr >> 3) * 8), 0)

    @pl.loop(0, 2)
    def _(t):
        ids = lax.broadcasted_iota(jnp.int32, (64, 256), 0) + t * 64
        total = jnp.zeros((64, 256), jnp.int32)
        for p in range(64):
            total = total + jnp.where(pos[p:p + 1, :] == ids, field[p:p + 1, :], 0)
        for i in range(4):
            part = (total >> (8 * i)) & 255
            counts[rows_at(i * 128 + t * 64, 64), :] = part.astype(F32).astype(BF16)

    for t in range(2):
        cols = slice(t * 512, t * 512 + 512)
        partial[:, cols] = lax.dot_general(counts[...], tokens[:, cols], TN, preferred_element_type=F32)

    pair = pltpu.make_async_remote_copy(
        src_ref=partial.at[rows_at((1 - core) * 128, 128)], dst_ref=buf0, send_sem=s0, recv_sem=r0,
        device_id=(ns + 1 - 2 * core, ew), device_id_type=MESH)
    pair.start()

    def project(weight, bias_at, dst, place):
        size = 128 * len(place)
        for n in range(2):
            cols = slice(n * 512, n * 512 + 512)
            y = jnp.dot(normed[0:size, :], weight[:, cols], preferred_element_type=F32)
            y = (y + wb[:, bias_at + n * 512:bias_at + n * 512 + 512]).astype(BF16)
            for i, at in enumerate(place):
                dst[at:at + 128, cols] = y[i * 128:i * 128 + 128]

    def norm_into(at, x):
        normed[at:at + x.shape[0], :] = norm_rows(x.astype(F32), gain[...], beta[...]).astype(BF16)

    for c in loads[6:]:
        c.wait()
    for i in range(2):
        norm_into(i * 256, tokens[i * 256:i * 256 + 256, :])

    mid_own = (256, 512, 768, 1024)
    mid_side = (384, 640, 896, 1152)
    loads[2].wait()
    project(wk, 1024, k, mid_own)
    pair.wait()

    @pl.loop(0, 8)
    def _(t):
        p1[t] = partial[rows_at(core * 128 + t * 16, 16), :] + buf0[rows_at(t * 16, 16), :]

    def stage1(d):
        to = lax.rem(unit + d, 8)
        return pltpu.make_async_remote_copy(src_ref=p1.at[to], dst_ref=buf1.at[d], send_sem=s1.at[d], recv_sem=r1.at[d],
                                            device_id=(to * 2 + core, ew), device_id_type=MESH)
    pl.loop(1, 8)(lambda d: stage1(d).start())

    loads[3].wait()
    project(wv, 2048, v, mid_own)

    low = lax.broadcasted_iota(jnp.int32, (128, 128), 1) < 64
    loads[4].wait()

    for n in range(2):
        cols = slice(n * 512, n * 512 + 512)
        y = jnp.dot(normed[...], wq[:, cols], preferred_element_type=F32)
        y = (y + wb[:, cols]).astype(BF16).astype(F32) * 0.125
        for b in range(4):
            for i in range(4):
                q = y[b * 128:b * 128 + 128, i * 128:i * 128 + 128]
                q2[n * 4 + i, b * 256:b * 256 + 128, :] = jnp.where(low, q, 0.0).astype(BF16)
                q2[n * 4 + i, b * 256 + 128:b * 256 + 256, :] = jnp.where(low, 0.0, q).astype(BF16)

    pl.when(has_down)(go_up[0].wait_recv)
    pl.when(has_up)(go_down[0].wait_recv)
    norm_into(0, rim[0, 0:128, :])
    norm_into(128, rim[5, 0:128, :])
    project(wk, 1024, k, (0, 1280))
    project(wv, 2048, v, (0, 1280))

    for i in range(2):
        pl.when(has_left)(go_right[i].wait_recv)
        pl.when(has_right)(go_left[i].wait_recv)
    when_all(has_left & has_up, [west_up.start])
    when_all(has_left & has_down, [west_down.start])
    when_all(has_right & has_up, [east_up.start])
    when_all(has_right & has_down, [east_down.start])
    pl.when(has_left)(go_right[2].wait_recv)
    pl.when(has_right)(go_left[2].wait_recv)

    pl.loop(1, 8)(lambda d: stage1(d).wait())
    total = p1[unit]
    for d in range(1, 8):
        total = total + buf1[d]
    for i in range(8):
        p2[:, i, :] = total[:, i * 128:i * 128 + 128]

    def stage2(d):
        to = lax.rem(ew + d, 16)
        return pltpu.make_async_remote_copy(src_ref=p2.at[to], dst_ref=buf2.at[d], send_sem=s2.at[d], recv_sem=r2.at[d],
                                            device_id=(ns, to), device_id_type=MESH)
    pl.loop(1, 16)(lambda d: stage2(d).start())

    for i in range(4):
        norm_into(i * 128, rim[i + 1, 128:256, :])
    project(wk, 1024, k, mid_side)
    project(wv, 2048, v, mid_side)

    def stage3(d):
        return pltpu.make_async_remote_copy(src_ref=g.at[ew], dst_ref=g.at[ew], send_sem=s3.at[d], recv_sem=r3.at[d],
                                            device_id=(ns, lax.rem(ew + d, 16)), device_id_type=MESH)

    def stage3_in(d):
        at = lax.rem(ew + 16 - d, 16)
        return pltpu.make_async_remote_copy(src_ref=g.at[at], dst_ref=g.at[at], send_sem=s3.at[d], recv_sem=r3.at[d],
                                            device_id=(ns, at), device_id_type=MESH)

    def stage4(d):
        mine = ctx.at[core, unit]
        return pltpu.make_async_remote_copy(src_ref=mine, dst_ref=mine, send_sem=s4.at[d], recv_sem=r4.at[d],
                                            device_id=(lax.rem(ns + d, 16), ew), device_id_type=MESH)

    def stage4_in(d):
        at = lax.rem(ns + 16 - d, 16)
        theirs = ctx.at[lax.rem(at, 2), at // 2]
        return pltpu.make_async_remote_copy(src_ref=theirs, dst_ref=theirs, send_sem=s4.at[d], recv_sem=r4.at[d],
                                            device_id=(at, ew), device_id_type=MESH)

    s_buf, p_buf, ml_buf = (s_a, s_b), (p_a, p_b), (ml_a, ml_b)

    def soft_rows(s, bias, pb, mlb, at, size):
        rows = slice(at, at + size)
        x = s[rows, :]
        if bias is not None:
            x = x + bias[at % 128:at % 128 + size, :]
        m = jnp.max(x, axis=1, keepdims=True)
        e = jnp.exp(x - m)
        l = jnp.sum(e, axis=1, keepdims=True)
        pb[rows, :] = e.astype(BF16)
        mlb[0, rows, :] = jnp.broadcast_to(m, (size, 128))
        mlb[1, rows, :] = jnp.broadcast_to(l, (size, 128))

    def band_step(t):
        b = lax.rem(t + 1, 4)
        for j in range(6):
            qi = lax.broadcasted_iota(jnp.int32, (128, 128), 0)
            ki = lax.broadcasted_iota(jnp.int32, (128, 128), 1)
            qr = 8 + qi // 16
            qc = 8 + qi % 16
            if j % 2 == 0:
                kr = 8 * (j // 2) + ki // 16
                kc_ = 8 + ki % 16
            else:
                kr = 8 * (j // 2) + (ki % 64) // 8
                kc_ = ki % 8 + jnp.where(ki < 64, 0, 24)
            gr = ns * 32 + 8 * b - 8 + kr
            gc = ew * 16 - 8 + kc_
            ok = ((kr - qr <= 7) & (qr - kr <= 7) & (kc_ - qc <= 7) & (qc - kc_ <= 7)
                  & (gr >= 0) & (gr < 512) & (gc >= 0) & (gc < 256))
            near_bias[:, j * 128:j * 128 + 128] = jnp.where(ok, 0.0, -1e30)

        qrows = rows_at(b * 128, 128)

        def keys(part):
            return rows_at(b * 256 + part * 256, 256)

        def scores(p, part):
            lanes = slice(p * 128, p * 128 + 128)
            s_buf[p % 2][:, part * 256:part * 256 + 256] = lax.dot_general(
                q2[p, rows_at(b * 256, 256), :], k[keys(part), lanes], NT, preferred_element_type=F32)

        for part in range(3):
            scores(0, part)
        for u in range(9):
            o = None
            for part in range(3):
                if u + 1 < 8:
                    scores(u + 1, part)
                if u > 0:
                    lanes = slice((u - 1) * 128, u * 128)
                    term = jnp.dot(p_buf[(u - 1) % 2][:, part * 256:part * 256 + 256], v[keys(part), lanes],
                                   preferred_element_type=F32)
                    o = term if o is None else o + term
                if u < 8:
                    for r in ((0, 5), (5, 10), (10, 16))[part:part + 1]:
                        for c in range(*r):
                            soft_rows(s_buf[u % 2], near_bias, p_buf[u % 2], ml_buf[u % 2], c * 16, 16)
            if u > 0:
                mlb = ml_buf[(u - 1) % 2]
                near_o[qrows, lanes] = jnp.where(low, o[0:128], o[128:256])
                near_m[qrows, lanes] = jnp.where(low, mlb[0, 0:128], mlb[0, 128:256])
                near_l[qrows, lanes] = jnp.where(low, mlb[1, 0:128], mlb[1, 128:256])

    pl.loop(1, 16)(lambda d: stage2(d).wait())
    total = p2[ew]
    for d in range(1, 16):
        total = total + buf2[d]
    g[ew] = total
    pl.loop(1, 16)(lambda d: stage3(d).start())

    @pl.loop(0, 4)
    def _(t):
        @pl.when(t == 2)
        def _():
            when_all(has_left & has_down, [west_up.wait_recv])
            when_all(has_left & has_up, [west_down.wait_recv])
            when_all(has_right & has_down, [east_up.wait_recv])
            when_all(has_right & has_up, [east_down.wait_recv])

            norm_into(0, rim[0, 128:256, :])
            norm_into(128, rim[5, 128:256, :])
            project(wk, 1024, k, (128, 1408))
            project(wv, 2048, v, (128, 1408))

        band_step(t)

        @pl.when(t == 1)
        def _():
            @pl.loop(1, 16)
            def _(d):
                stage3(d).wait_send()
                stage3_in(d).wait_recv()

            pooled = jnp.concatenate([g[:, i, :] for i in range(8)], axis=1)
            ctx[core, unit] = norm_rows(pooled, cgain[...], cbias[...]).astype(BF16)
            pl.loop(1, 16)(lambda d: stage4(d).start())

    @pl.loop(1, 16)
    def _(d):
        stage4(d).wait_send()
        stage4_in(d).wait_recv()

    for i in range(2):
        for j in range(8):
            at = i * 128 + j * 16
            normed[at:at + 16, :] = ctx[i, j]
    ctx_out[...] = normed[0:256, :]

    project(wk, 1024, kc, (0, 128))
    project(wv, 2048, vc, (0, 128))

    def context_pair(p, cs, cp, cml):
        lanes = rows_at(p * 128, 128)
        for half in range(2):
            cs[half * 512:half * 512 + 512, :] = lax.dot_general(
                q2[p, half * 512:half * 512 + 512, :], kc[:, lanes], NT, preferred_element_type=F32)
        for c in range(32):
            soft_rows(cs, None, cp, cml, c * 32, 32)
        o = jnp.dot(cp[...], vc[:, lanes], preferred_element_type=F32)
        for b in range(4):
            a0, a1 = slice(b * 256, b * 256 + 128), slice(b * 256 + 128, b * 256 + 256)
            rows = slice(b * 128, b * 128 + 128)
            oc = jnp.where(low, o[a0], o[a1])
            mc = jnp.where(low, cml[0, a0, :], cml[0, a1, :])
            lc = jnp.where(low, cml[1, a0, :], cml[1, a1, :])
            mn = near_m[rows, lanes]
            m = jnp.maximum(mn, mc)
            fn, fc = jnp.exp(mn - m), jnp.exp(mc - m)
            both = near_o[rows, lanes] * fn + oc * fc
            att[rows, lanes] = (both / (near_l[rows, lanes] * fn + lc * fc)).astype(BF16)

    @pl.loop(0, 4)
    def _(i):
        context_pair(i * 2, cs, cp, cml)
        context_pair(i * 2 + 1, cs2, cp2, cml2)

    loads[5].wait()

    for n in range(2):
        cols = slice(n * 512, n * 512 + 512)
        y = jnp.dot(att[...], wo[:, cols], preferred_element_type=F32)
        out[:, cols] = (tokens[:, cols].astype(F32) + y + ob[:, cols]).astype(BF16)

    when_all(has_left, [c.wait_send for c in go_left])
    when_all(has_right, [c.wait_send for c in go_right])
    when_all(has_up, [go_up[0].wait_send])
    when_all(has_down, [go_down[0].wait_send])
    when_all(has_left & has_up, [west_up.wait_send])
    when_all(has_left & has_down, [west_down.wait_send])
    when_all(has_right & has_up, [east_up.wait_send])
    when_all(has_right & has_down, [east_down.wait_send])


def on_device(tokens, norm_gain, norm_bias, projection_weight, projection_bias, context_gain, context_bias,
              output_weight, output_bias, context_positions):
    vm = pl.BlockSpec(memory_space=pltpu.VMEM)
    hbm = pl.BlockSpec(memory_space=pltpu.MemorySpace.HBM)
    dma = pltpu.SemaphoreType.DMA

    def f32(*shape):
        return pltpu.VMEM(shape, F32)

    def b16(*shape):
        return pltpu.VMEM(shape, BF16)

    mixed, context = pl.pallas_call(
        layer,
        out_shape=(jax.ShapeDtypeStruct((512, 1024), BF16), jax.ShapeDtypeStruct((256, 1024), BF16)),
        in_specs=[hbm] * 10,
        out_specs=(vm, vm),
        scratch_shapes=[
            f32(1, 1024), f32(1, 1024), f32(1, 3072), f32(1, 1024), f32(1, 1024), f32(1, 1024),
            b16(512, 1024), pltpu.VMEM((64, 256), jnp.int32), pltpu.VMEM((64, 256), jnp.int32), b16(1024, 1024), b16(1024, 1024), b16(1024, 1024),
            b16(1024, 1024), b16(512, 1024), b16(1536, 1024), b16(1536, 1024), b16(8, 1024, 128), b16(512, 1024),
            f32(512, 1024), f32(512, 1024), f32(512, 1024), f32(128, 768),
            f32(256, 768), f32(256, 768), b16(256, 768), b16(256, 768), f32(2, 256, 128), f32(2, 256, 128),
            f32(1024, 256), b16(1024, 256), f32(2, 1024, 128), f32(1024, 256), b16(1024, 256), f32(2, 1024, 128), b16(256, 1024), b16(256, 1024), b16(2, 8, 16, 1024),
            b16(6, 256, 1024), b16(4, 64, 1024), b16(4, 64, 1024),
            b16(512, 256), f32(256, 1024), f32(128, 1024), f32(8, 16, 1024), f32(8, 16, 1024),
            f32(16, 8, 128), f32(16, 8, 128), f32(16, 8, 128),
            dma((12,)), dma((12,)), dma((12,)), dma, dma, dma((8,)), dma((8,)),
            dma((16,)), dma((16,)), dma((16,)), dma((16,)), dma((16,)), dma((16,)),
        ],
        compiler_params=pltpu.CompilerParams(collective_id=0, has_side_effects=True, vmem_limit_bytes=50 * 2**20),
        name="layer",
    )(*[pltpu.with_memory_space_constraint(a, pltpu.MemorySpace.HBM) for a in (
        tokens.reshape(512, 1024), context_positions.T, projection_weight, output_weight,
        norm_gain.reshape(1, -1), norm_bias.reshape(1, -1), projection_bias.reshape(1, -1),
        context_gain.reshape(1, -1), context_bias.reshape(1, -1), output_bias.reshape(1, -1))])
    return mixed.reshape(32, 16, 1024), context


def solution(mesh):
    return jax.shard_map(
        on_device,
        mesh=mesh,
        in_specs=(P("ns", "ew", None), P(), P(), P(), P(), P(), P(), P(), P(), P()),
        out_specs=(P("ns", "ew", None), P()),
        check_vma=False,
    )
```

```python
import jax
import jax.numpy as jnp
from jax import lax
from jax.experimental import pallas as pl
from jax.experimental.pallas import tpu as pltpu
from jax.sharding import PartitionSpec as P

F32 = jnp.float32
BF16 = jnp.bfloat16
MESH = pl.DeviceIdType.MESH
NT = (((1,), (1,)), ((), ()))
TN = (((0,), (0,)), ((), ()))


def rows_at(start, size):
    return pl.ds(pl.multiple_of(start, size), size)


def norm_rows(x, gain, bias):
    centre = x - jnp.mean(x, axis=-1, keepdims=True)
    spread = jnp.mean(centre * centre, axis=-1, keepdims=True)
    return centre * lax.rsqrt(spread + 1e-05) * gain + bias


def layer(tokens_hbm, pos_hbm, w_hbm, wo_hbm, gain_hbm, beta_hbm, wb_hbm, cgain_hbm, cbias_hbm, ob_hbm, out, ctx_out,
          gain, beta, wb, cgain, cbias, ob, tokens, pos, field, wq, wk, wv, wo, normed, k, v, q2, att, near_o, near_m, near_l, near_bias,
          s_a, s_b, p_a, p_b, ml_a, ml_b, cs, cp, cml, cs2, cp2, cml2, kc, vc, ctx,
          rim, send_l, send_r, counts, partial, buf0, p1, buf1, p2, buf2, g,
          load, halo_s, halo_r, s0, r0, s1, r1, s2, r2, s3, r3, s4, r4):
    ns = lax.axis_index("ns")
    ew = lax.axis_index("ew")
    core = lax.rem(ns, 2)
    unit = ns // 2

    barrier = pltpu.get_barrier_semaphore()

    @pl.loop(1, 16)
    def _(d):
        pl.semaphore_signal(barrier, inc=1, device_id=(lax.rem(ns + d, 16), ew), device_id_type=MESH)
        pl.semaphore_signal(barrier, inc=1, device_id=(ns, lax.rem(ew + d, 16)), device_id_type=MESH)

    loads = [pltpu.make_async_copy(a, b, load.at[i]) for i, (a, b) in enumerate((
        (tokens_hbm, tokens), (pos_hbm, pos), (w_hbm.at[:, pl.ds(1024, 1024)], wk), (w_hbm.at[:, pl.ds(2048, 1024)], wv),
        (w_hbm.at[:, pl.ds(0, 1024)], wq), (wo_hbm, wo), (gain_hbm, gain), (beta_hbm, beta), (wb_hbm, wb),
        (cgain_hbm, cgain), (cbias_hbm, cbias), (ob_hbm, ob)))]
    for c in loads[:2] + loads[6:] + loads[2:6]:
        c.start()
    loads[0].wait()

    @pl.loop(0, 4)
    def _(b):
        x = tokens[rows_at(b * 128, 128), :].astype(F32).reshape(8, 2, 8, 1024)
        send_l[b] = x[:, 0].reshape(64, 1024).astype(BF16)
        send_r[b] = x[:, 1].reshape(64, 1024).astype(BF16)

    up, down, left, right = (ns - 1, ew), (ns + 1, ew), (ns, ew - 1), (ns, ew + 1)

    def halo(i, src, dst, device):
        return pltpu.make_async_remote_copy(src_ref=src, dst_ref=dst, send_sem=halo_s.at[i], recv_sem=halo_r.at[i],
                                            device_id=device, device_id_type=MESH)
    west, east = pl.ds(128, 64), pl.ds(192, 64)
    go_left = [halo(0, send_l.at[0], rim.at[1, east], left), halo(1, send_l.at[3], rim.at[4, east], left),
               halo(2, send_l.at[pl.ds(1, 2)], rim.at[pl.ds(2, 2), east], left)]
    go_right = [halo(3, send_r.at[0], rim.at[1, west], right), halo(4, send_r.at[3], rim.at[4, west], right),
                halo(5, send_r.at[pl.ds(1, 2)], rim.at[pl.ds(2, 2), west], right)]
    go_up = [halo(6, tokens.at[pl.ds(0, 128)], rim.at[5, pl.ds(0, 128)], up)]
    go_down = [halo(7, tokens.at[pl.ds(384, 128)], rim.at[0, pl.ds(0, 128)], down)]
    west_up = halo(8, rim.at[1, west], rim.at[5, west], up)
    west_down = halo(9, rim.at[4, west], rim.at[0, west], down)
    east_up = halo(10, rim.at[1, east], rim.at[5, east], up)
    east_down = halo(11, rim.at[4, east], rim.at[0, east], down)
    has_up, has_down, has_left, has_right = ns > 0, ns < 15, ew > 0, ew < 15

    def when_all(cond, calls):
        @pl.when(cond)
        def _():
            for c in calls:
                c()

    pl.semaphore_wait(barrier, 30)
    pl.when(has_up)(go_up[0].start)
    pl.when(has_down)(go_down[0].start)
    for i in range(3):
        pl.when(has_left)(go_left[i].start)
        pl.when(has_right)(go_right[i].start)

    @pl.when(jnp.logical_not(has_up))
    def _():
        rim[0] = jnp.zeros((256, 1024), BF16)

    @pl.when(jnp.logical_not(has_down))
    def _():
        rim[5] = jnp.zeros((256, 1024), BF16)

    for gone, at in ((ew == 0, 128), (ew == 15, 192)):
        @pl.when(gone)
        def _():
            @pl.loop(0, 6)
            def _(t):
                rim[t, at:at + 64, :] = jnp.zeros((64, 1024), BF16)

    loads[1].wait()
    lr = (pos[...] >> 8) - ns * 32
    lc = (pos[...] & 255) - ew * 16
    own = (lr >= 0) & (lr < 32) & (lc >= 0) & (lc < 16)
    pos[...] = jnp.where(own, (lr & 7) * 16 + lc, -1)
    field[...] = jnp.where(own, lax.shift_left(jnp.ones_like(lr), (lr >> 3) * 8), 0)

    @pl.loop(0, 2)
    def _(t):
        ids = lax.broadcasted_iota(jnp.int32, (64, 256), 0) + t * 64
        total = jnp.zeros((64, 256), jnp.int32)
        for p in range(64):
            total = total + jnp.where(pos[p:p + 1, :] == ids, field[p:p + 1, :], 0)
        for i in range(4):
            part = (total >> (8 * i)) & 255
            counts[rows_at(i * 128 + t * 64, 64), :] = part.astype(F32).astype(BF16)

    for t in range(2):
        cols = slice(t * 512, t * 512 + 512)
        partial[:, cols] = lax.dot_general(counts[...], tokens[:, cols], TN, preferred_element_type=F32)

    pair = pltpu.make_async_remote_copy(
        src_ref=partial.at[rows_at((1 - core) * 128, 128)], dst_ref=buf0, send_sem=s0, recv_sem=r0,
        device_id=(ns + 1 - 2 * core, ew), device_id_type=MESH)
    pair.start()

    def project(weight, bias_at, dst, place):
        size = 128 * len(place)
        for n in range(2):
            cols = slice(n * 512, n * 512 + 512)
            y = jnp.dot(normed[0:size, :], weight[:, cols], preferred_element_type=F32)
            y = (y + wb[:, bias_at + n * 512:bias_at + n * 512 + 512]).astype(BF16)
            for i, at in enumerate(place):
                dst[at:at + 128, cols] = y[i * 128:i * 128 + 128]

    def norm_into(at, x):
        normed[at:at + x.shape[0], :] = norm_rows(x.astype(F32), gain[...], beta[...]).astype(BF16)

    for c in loads[6:]:
        c.wait()
    for i in range(2):
        norm_into(i * 256, tokens[i * 256:i * 256 + 256, :])

    mid_own = (256, 512, 768, 1024)
    mid_side = (384, 640, 896, 1152)
    loads[2].wait()
    project(wk, 1024, k, mid_own)
    pair.wait()

    @pl.loop(0, 8)
    def _(t):
        p1[t] = partial[rows_at(core * 128 + t * 16, 16), :] + buf0[rows_at(t * 16, 16), :]

    def stage1(d):
        to = lax.rem(unit + d, 8)
        return pltpu.make_async_remote_copy(src_ref=p1.at[to], dst_ref=buf1.at[d], send_sem=s1.at[d], recv_sem=r1.at[d],
                                            device_id=(to * 2 + core, ew), device_id_type=MESH)
    pl.loop(1, 8)(lambda d: stage1(d).start())

    loads[3].wait()
    project(wv, 2048, v, mid_own)

    low = lax.broadcasted_iota(jnp.int32, (128, 128), 1) < 64
    loads[4].wait()

    for n in range(2):
        cols = slice(n * 512, n * 512 + 512)
        y = jnp.dot(normed[...], wq[:, cols], preferred_element_type=F32)
        y = (y + wb[:, cols]).astype(BF16).astype(F32) * 0.125
        for b in range(4):
            for i in range(4):
                q = y[b * 128:b * 128 + 128, i * 128:i * 128 + 128]
                q2[n * 4 + i, b * 256:b * 256 + 128, :] = jnp.where(low, q, 0.0).astype(BF16)
                q2[n * 4 + i, b * 256 + 128:b * 256 + 256, :] = jnp.where(low, 0.0, q).astype(BF16)

    pl.when(has_down)(go_up[0].wait_recv)
    pl.when(has_up)(go_down[0].wait_recv)
    norm_into(0, rim[0, 0:128, :])
    norm_into(128, rim[5, 0:128, :])
    project(wk, 1024, k, (0, 1280))
    project(wv, 2048, v, (0, 1280))

    for i in range(2):
        pl.when(has_left)(go_right[i].wait_recv)
        pl.when(has_right)(go_left[i].wait_recv)
    when_all(has_left & has_up, [west_up.start])
    when_all(has_left & has_down, [west_down.start])
    when_all(has_right & has_up, [east_up.start])
    when_all(has_right & has_down, [east_down.start])
    pl.when(has_left)(go_right[2].wait_recv)
    pl.when(has_right)(go_left[2].wait_recv)

    pl.loop(1, 8)(lambda d: stage1(d).wait())
    total = p1[unit]
    for d in range(1, 8):
        total = total + buf1[d]
    for i in range(8):
        p2[:, i, :] = total[:, i * 128:i * 128 + 128]

    def stage2(d):
        to = lax.rem(ew + d, 16)
        return pltpu.make_async_remote_copy(src_ref=p2.at[to], dst_ref=buf2.at[d], send_sem=s2.at[d], recv_sem=r2.at[d],
                                            device_id=(ns, to), device_id_type=MESH)
    pl.loop(1, 16)(lambda d: stage2(d).start())

    for i in range(4):
        norm_into(i * 128, rim[i + 1, 128:256, :])
    project(wk, 1024, k, mid_side)
    project(wv, 2048, v, mid_side)

    def stage3(d):
        return pltpu.make_async_remote_copy(src_ref=g.at[ew], dst_ref=g.at[ew], send_sem=s3.at[d], recv_sem=r3.at[d],
                                            device_id=(ns, lax.rem(ew + d, 16)), device_id_type=MESH)

    def stage3_in(d):
        at = lax.rem(ew + 16 - d, 16)
        return pltpu.make_async_remote_copy(src_ref=g.at[at], dst_ref=g.at[at], send_sem=s3.at[d], recv_sem=r3.at[d],
                                            device_id=(ns, at), device_id_type=MESH)

    def stage4(d):
        mine = ctx.at[core, unit]
        return pltpu.make_async_remote_copy(src_ref=mine, dst_ref=mine, send_sem=s4.at[d], recv_sem=r4.at[d],
                                            device_id=(lax.rem(ns + d, 16), ew), device_id_type=MESH)

    def stage4_in(d):
        at = lax.rem(ns + 16 - d, 16)
        theirs = ctx.at[lax.rem(at, 2), at // 2]
        return pltpu.make_async_remote_copy(src_ref=theirs, dst_ref=theirs, send_sem=s4.at[d], recv_sem=r4.at[d],
                                            device_id=(at, ew), device_id_type=MESH)

    s_buf, p_buf, ml_buf = (s_a, s_b), (p_a, p_b), (ml_a, ml_b)

    def soft_rows(s, bias, pb, mlb, at, size):
        rows = slice(at, at + size)
        x = s[rows, :]
        if bias is not None:
            x = x + bias[at % 128:at % 128 + size, :]
        m = jnp.max(x, axis=1, keepdims=True)
        e = jnp.exp(x - m)
        l = jnp.sum(e, axis=1, keepdims=True)
        pb[rows, :] = e.astype(BF16)
        mlb[0, rows, :] = jnp.broadcast_to(m, (size, 128))
        mlb[1, rows, :] = jnp.broadcast_to(l, (size, 128))

    def band_step(t):
        b = lax.rem(t + 1, 4)
        for j in range(6):
            qi = lax.broadcasted_iota(jnp.int32, (128, 128), 0)
            ki = lax.broadcasted_iota(jnp.int32, (128, 128), 1)
            qr = 8 + qi // 16
            qc = 8 + qi % 16
            if j % 2 == 0:
                kr = 8 * (j // 2) + ki // 16
                kc_ = 8 + ki % 16
            else:
                kr = 8 * (j // 2) + (ki % 64) // 8
                kc_ = ki % 8 + jnp.where(ki < 64, 0, 24)
            gr = ns * 32 + 8 * b - 8 + kr
            gc = ew * 16 - 8 + kc_
            ok = ((kr - qr <= 7) & (qr - kr <= 7) & (kc_ - qc <= 7) & (qc - kc_ <= 7)
                  & (gr >= 0) & (gr < 512) & (gc >= 0) & (gc < 256))
            near_bias[:, j * 128:j * 128 + 128] = jnp.where(ok, 0.0, -1e30)

        qrows = rows_at(b * 128, 128)

        def keys(part):
            return rows_at(b * 256 + part * 256, 256)

        def scores(p, part):
            lanes = slice(p * 128, p * 128 + 128)
            s_buf[p % 2][:, part * 256:part * 256 + 256] = lax.dot_general(
                q2[p, rows_at(b * 256, 256), :], k[keys(part), lanes], NT, preferred_element_type=F32)

        for part in range(3):
            scores(0, part)
        for u in range(9):
            o = None
            for part in range(3):
                if u + 1 < 8:
                    scores(u + 1, part)
                if u > 0:
                    lanes = slice((u - 1) * 128, u * 128)
                    term = jnp.dot(p_buf[(u - 1) % 2][:, part * 256:part * 256 + 256], v[keys(part), lanes],
                                   preferred_element_type=F32)
                    o = term if o is None else o + term
                if u < 8:
                    for r in ((0, 5), (5, 10), (10, 16))[part:part + 1]:
                        for c in range(*r):
                            soft_rows(s_buf[u % 2], near_bias, p_buf[u % 2], ml_buf[u % 2], c * 16, 16)
            if u > 0:
                mlb = ml_buf[(u - 1) % 2]
                near_o[qrows, lanes] = jnp.where(low, o[0:128], o[128:256])
                near_m[qrows, lanes] = jnp.where(low, mlb[0, 0:128], mlb[0, 128:256])
                near_l[qrows, lanes] = jnp.where(low, mlb[1, 0:128], mlb[1, 128:256])

    pl.loop(1, 16)(lambda d: stage2(d).wait())
    total = p2[ew]
    for d in range(1, 16):
        total = total + buf2[d]
    g[ew] = total
    pl.loop(1, 16)(lambda d: stage3(d).start())

    @pl.loop(0, 4)
    def _(t):
        @pl.when(t == 2)
        def _():
            when_all(has_left & has_down, [west_up.wait_recv])
            when_all(has_left & has_up, [west_down.wait_recv])
            when_all(has_right & has_down, [east_up.wait_recv])
            when_all(has_right & has_up, [east_down.wait_recv])

            norm_into(0, rim[0, 128:256, :])
            norm_into(128, rim[5, 128:256, :])
            project(wk, 1024, k, (128, 1408))
            project(wv, 2048, v, (128, 1408))

        band_step(t)

        @pl.when(t == 1)
        def _():
            @pl.loop(1, 16)
            def _(d):
                stage3(d).wait_send()
                stage3_in(d).wait_recv()

            pooled = jnp.concatenate([g[:, i, :] for i in range(8)], axis=1)
            ctx[core, unit] = norm_rows(pooled, cgain[...], cbias[...]).astype(BF16)
            pl.loop(1, 16)(lambda d: stage4(d).start())

    @pl.loop(1, 16)
    def _(d):
        stage4(d).wait_send()
        stage4_in(d).wait_recv()

    for i in range(2):
        for j in range(8):
            at = i * 128 + j * 16
            normed[at:at + 16, :] = ctx[i, j]
    ctx_out[...] = normed[0:256, :]

    project(wk, 1024, kc, (0, 128))
    project(wv, 2048, vc, (0, 128))

    def context_pair(p, cs, cp, cml):
        lanes = rows_at(p * 128, 128)
        for half in range(2):
            cs[half * 512:half * 512 + 512, :] = lax.dot_general(
                q2[p, half * 512:half * 512 + 512, :], kc[:, lanes], NT, preferred_element_type=F32)
        for c in range(32):
            soft_rows(cs, None, cp, cml, c * 32, 32)
        o = jnp.dot(cp[...], vc[:, lanes], preferred_element_type=F32)
        for b in range(4):
            a0, a1 = slice(b * 256, b * 256 + 128), slice(b * 256 + 128, b * 256 + 256)
            rows = slice(b * 128, b * 128 + 128)
            oc = jnp.where(low, o[a0], o[a1])
            mc = jnp.where(low, cml[0, a0, :], cml[0, a1, :])
            lc = jnp.where(low, cml[1, a0, :], cml[1, a1, :])
            mn = near_m[rows, lanes]
            m = jnp.maximum(mn, mc)
            fn, fc = jnp.exp(mn - m), jnp.exp(mc - m)
            both = near_o[rows, lanes] * fn + oc * fc
            att[rows, lanes] = (both / (near_l[rows, lanes] * fn + lc * fc)).astype(BF16)

    @pl.loop(0, 4)
    def _(i):
        context_pair(i * 2, cs, cp, cml)
        context_pair(i * 2 + 1, cs2, cp2, cml2)

    loads[5].wait()

    for n in range(2):
        cols = slice(n * 512, n * 512 + 512)
        y = jnp.dot(att[...], wo[:, cols], preferred_element_type=F32)
        out[:, cols] = (tokens[:, cols].astype(F32) + y + ob[:, cols]).astype(BF16)

    when_all(has_left, [c.wait_send for c in go_left])
    when_all(has_right, [c.wait_send for c in go_right])
    when_all(has_up, [go_up[0].wait_send])
    when_all(has_down, [go_down[0].wait_send])
    when_all(has_left & has_up, [west_up.wait_send])
    when_all(has_left & has_down, [west_down.wait_send])
    when_all(has_right & has_up, [east_up.wait_send])
    when_all(has_right & has_down, [east_down.wait_send])


def on_device(tokens, norm_gain, norm_bias, projection_weight, projection_bias, context_gain, context_bias,
              output_weight, output_bias, context_positions):
    vm = pl.BlockSpec(memory_space=pltpu.VMEM)
    hbm = pl.BlockSpec(memory_space=pltpu.MemorySpace.HBM)
    dma = pltpu.SemaphoreType.DMA

    def f32(*shape):
        return pltpu.VMEM(shape, F32)

    def b16(*shape):
        return pltpu.VMEM(shape, BF16)

    mixed, context = pl.pallas_call(
        layer,
        out_shape=(jax.ShapeDtypeStruct((512, 1024), BF16), jax.ShapeDtypeStruct((256, 1024), BF16)),
        in_specs=[hbm] * 10,
        out_specs=(vm, vm),
        scratch_shapes=[
            f32(1, 1024), f32(1, 1024), f32(1, 3072), f32(1, 1024), f32(1, 1024), f32(1, 1024),
            b16(512, 1024), pltpu.VMEM((64, 256), jnp.int32), pltpu.VMEM((64, 256), jnp.int32), b16(1024, 1024), b16(1024, 1024), b16(1024, 1024),
            b16(1024, 1024), b16(512, 1024), b16(1536, 1024), b16(1536, 1024), b16(8, 1024, 128), b16(512, 1024),
            f32(512, 1024), f32(512, 1024), f32(512, 1024), f32(128, 768),
            f32(256, 768), f32(256, 768), b16(256, 768), b16(256, 768), f32(2, 256, 128), f32(2, 256, 128),
            f32(1024, 256), b16(1024, 256), f32(2, 1024, 128), f32(1024, 256), b16(1024, 256), f32(2, 1024, 128), b16(256, 1024), b16(256, 1024), b16(2, 8, 16, 1024),
            b16(6, 256, 1024), b16(4, 64, 1024), b16(4, 64, 1024),
            b16(512, 256), f32(256, 1024), f32(128, 1024), f32(8, 16, 1024), f32(8, 16, 1024),
            f32(16, 8, 128), f32(16, 8, 128), f32(16, 8, 128),
            dma((12,)), dma((12,)), dma((12,)), dma, dma, dma((8,)), dma((8,)),
            dma((16,)), dma((16,)), dma((16,)), dma((16,)), dma((16,)), dma((16,)),
        ],
        compiler_params=pltpu.CompilerParams(collective_id=0, has_side_effects=True, vmem_limit_bytes=50 * 2**20),
        name="layer",
    )(*[pltpu.with_memory_space_constraint(a, pltpu.MemorySpace.HBM) for a in (
        tokens.reshape(512, 1024), context_positions.T, projection_weight, output_weight,
        norm_gain.reshape(1, -1), norm_bias.reshape(1, -1), projection_bias.reshape(1, -1),
        context_gain.reshape(1, -1), context_bias.reshape(1, -1), output_bias.reshape(1, -1))])
    return mixed.reshape(32, 16, 1024), context


def solution(mesh):
    return jax.shard_map(
        on_device,
        mesh=mesh,
        in_specs=(P("ns", "ew", None), P(), P(), P(), P(), P(), P(), P(), P(), P()),
        out_specs=(P("ns", "ew", None), P()),
        check_vma=False,
    )
```
